256 devices in a mesh: box: 64 (over z, x_lo, y), snap: 4 (over x_hi, core).
Axes of the slice: x: 4 (x_hi: 2, x_lo: 2; x = x_hi * 2 + x_lo), y: 4, z: 8, core: 2. Of those that a mesh axis runs over, the one named last changes fastest.
Arguments:
- fields: bfloat16 [4, 320, 48, 1024], P('snap', 'box'), may hold values from -6 to 6
- cotangent: bfloat16 [4, 320, 48, 1024], P('snap', 'box'), may hold values from -0.0068359375 to 0.0068359375
- plane_counts: int32 [4, 64], P('snap', 'box'), may hold values from 2 to 5, as said below
- w_first: bfloat16 [48, 1296], replicated, may hold values from -0.15625 to 0.15625
- b_first: float32 [48], replicated, may hold values from -3 to 3
- w_second: bfloat16 [48, 1296], replicated, may hold values from -0.15625 to 0.15625
- b_second: float32 [48], replicated, may hold values from -3 to 3
Outputs:
- decoded: bfloat16 [4, 320, 48, 1024], P('snap', 'box')
- grad_first: float32 [48, 1296], replicated
- grad_second: float32 [48, 1296], replicated
- bias_grad_first: float32 [48], replicated
- bias_grad_second: float32 [48], replicated
The draws below stay inside these ranges and needn't reach their ends.
Inputs may be any that keep to these rules, and one draw needn't show every extreme that they name: `plane_counts`: in each snapshot every device holds 2 to 5 planes and the devices hold 184 planes together; a device's planes continue the chain right after those of the device before it along box.
All inputs are finite; a program needn't handle non-finite values.
Results may differ from the reference program's by a relative error of at most 0.008.
Values may be sent and summed in bfloat16 or wider, within the bound.
No kernel may reach another device: no remote copies, remote signals or barrier semaphores. Data moves between devices by JAX's collectives and lax.ppermute only.
A program may use at most 64 MiB of HBM per device.

```python
import jax
import jax.numpy as jnp
from jax import lax

C = 48
SIDE = 32
L_MAX = 5
SNAPS = 4
SLOTS = 320
PLANES = 184


def draw_plane_counts(key, part):
    device_total = SLOTS // L_MAX
    positions = jnp.arange(device_total, dtype=jnp.int32)
    eighth = device_total // 8
    quarter = device_total // 4
    extras = jnp.where(positions < eighth, L_MAX - 2, jnp.where(positions < eighth + quarter, 2, 0)).astype(jnp.int32)
    key_list = jax.random.split(key, SNAPS)
    shuffled = [jax.random.permutation(key_list[index], extras) for index in range(SNAPS)]
    return (2 + jnp.stack(shuffled)).astype(jnp.int32)


def steps_of(stream_key, dims, cuts, least, top_value):
    loudness, own = 1.0, jax.random.fold_in(stream_key, 6)
    for axis_at, parts in cuts:
        heights = jnp.exp(jax.random.uniform(jax.random.fold_in(own, axis_at), (parts,), jnp.float32, least / len(cuts), top_value / len(cuts)))
        loudness = loudness * jnp.repeat(heights, dims[axis_at] // parts).reshape([-1 if axis == axis_at else 1 for axis in range(len(dims))])
    return loudness


def gaussian(rng, extent, deviation, reach, shards=(), kind=jnp.bfloat16):
    level = steps_of(rng, extent, shards, -0.22, 0.18) if shards else 1.0
    values = jax.random.normal(rng, extent, jnp.float32) * deviation * level
    return jnp.minimum(jnp.maximum(values, -reach), reach).astype(kind)


def setup_inputs(seed: int = 0) -> dict:
    streams_of = jax.random.split(jax.random.key(seed), 8)
    return {
        "fields": gaussian(streams_of[0], (SNAPS, SLOTS, C, SIDE * SIDE), 1.0, 6.0, ((0, 4), (1, 64))),
        "cotangent": gaussian(streams_of[1], (SNAPS, SLOTS, C, SIDE * SIDE), (PLANES * SNAPS * SIDE * SIDE) ** -0.5, 0.0068359375, ((0, 4), (1, 64))),
        "plane_counts": draw_plane_counts(jax.random.fold_in(streams_of[7], 71), 0),
        "w_first": gaussian(streams_of[3], (C, 27 * C), (27 * C) ** -0.5, 0.15625),
        "b_first": gaussian(streams_of[4], (C,), 0.5, 3.0, (), jnp.float32),
        "w_second": gaussian(streams_of[5], (C, 27 * C), (27 * C) ** -0.5, 0.15625),
        "b_second": gaussian(streams_of[6], (C,), 0.5, 3.0, (), jnp.float32),
    }


def conv_forward(padded, kernel):
    width = kernel.shape[0]
    shaped = kernel.reshape(width, 3, 3, 3, width)
    return lax.conv_general_dilated(padded, shaped, (1, 1, 1), 'VALID', rhs_dilation=(2, 2, 2), dimension_numbers=('NDCHW', 'ODHWI', 'NDCHW'), preferred_element_type=jnp.float32)

def weight_grad(padded, upstream):
    width = upstream.shape[2]
    result = lax.conv_general_dilated(padded, upstream, (2, 2, 2), 'VALID', dimension_numbers=('CDNHW', 'IDOHW', 'CDHWN'), preferred_element_type=jnp.float32)
    return result.reshape(width, 27 * width)

def flipped(kernel):
    width = kernel.shape[0]
    shaped = kernel.reshape(width, 3, 3, 3, width)[:, ::-1, ::-1, ::-1, :]
    return jnp.transpose(shaped, (4, 1, 2, 3, 0)).reshape(width, 27 * width)

def silu_slope(value):
    sigma = jax.nn.sigmoid(value)
    return sigma * (1.0 + value * (1.0 - sigma))

def pad_chain(field):
    return jnp.pad(field, ((2, 2), (0, 0), (2, 2), (2, 2)))[None]

def reference(fields, cotangent, plane_counts, w_first, b_first, w_second, b_second):
    width = fields.shape[2]
    decoded_list = []
    grad_first = jnp.zeros((width, 27 * width), jnp.float32)
    grad_second = jnp.zeros((width, 27 * width), jnp.float32)
    bias_first = jnp.zeros((width,), jnp.float32)
    bias_second = jnp.zeros((width,), jnp.float32)
    for snapshot in range(SNAPS):
        counts_row = plane_counts[snapshot].astype(jnp.int32)
        ending = jnp.cumsum(counts_row).astype(jnp.int32)
        starting = ending - counts_row
        plane_ids = jnp.arange(PLANES, dtype=jnp.int32)
        owner = lax.optimization_barrier(jnp.sum((ending[None, :] <= plane_ids[:, None]).astype(jnp.int32), axis=1)).astype(jnp.int32)
        slot_rows = (owner * L_MAX + plane_ids - starting[owner]).astype(jnp.int32)
        chain = fields[snapshot][slot_rows].reshape(PLANES, width, SIDE, SIDE)
        upstream = cotangent[snapshot][slot_rows].reshape(PLANES, width, SIDE, SIDE)
        padded_input = pad_chain(chain)
        hidden_pre = conv_forward(padded_input, w_first)[0] + b_first[None, :, None, None]
        hidden = jax.nn.silu(hidden_pre).astype(jnp.bfloat16)
        padded_hidden = pad_chain(hidden)
        output = (conv_forward(padded_hidden, w_second)[0] + b_second[None, :, None, None]).astype(jnp.bfloat16)
        placed = jnp.zeros((SLOTS, width, SIDE * SIDE), jnp.bfloat16).at[slot_rows].set(output.reshape(PLANES, width, SIDE * SIDE))
        decoded_list.append(placed)
        grad_second = grad_second + weight_grad(padded_hidden, upstream[None])
        bias_second = bias_second + lax.optimization_barrier(jnp.sum(upstream.astype(jnp.float32), axis=(0, 2, 3)))
        hidden_grad = conv_forward(pad_chain(upstream), flipped(w_second))[0]
        pre_grad = (hidden_grad * silu_slope(hidden_pre)).astype(jnp.bfloat16)
        grad_first = grad_first + weight_grad(padded_input, pre_grad[None])
        bias_first = bias_first + lax.optimization_barrier(jnp.sum(pre_grad.astype(jnp.float32), axis=(0, 2, 3)))
    return (jnp.stack(decoded_list), grad_first, grad_second, bias_first, bias_second)
```

```python
import functools

import jax
import jax.numpy as jnp
from jax import lax
from jax.experimental import pallas as pl
from jax.experimental.pallas import tpu as pltpu
from jax.sharding import PartitionSpec as P

C = 48
SLOTS = 5
CELLS = 1024
ROWS = 3 * C
TAPS9 = 9 * C
WIDE = CELLS + 256
CHUNK = 256
F32 = jnp.float32
BF16 = jnp.bfloat16


def lane_masks():
    lane = lax.broadcasted_iota(jnp.int32, (C, 128), 1)
    col = lane % 32

    def pick(cond):
        return jnp.where(cond, 1.0, 0.0).astype(BF16)

    return pick(lane < 64), pick(lane >= 64), pick(col >= 2), pick(col < 30)


def roll(v, shift):
    return pltpu.roll(v, shift, 1)


def to_halves(v, masks):
    low, high = masks[:2]
    orig = [v[:, 128 * h : 128 * h + 128] for h in range(8)]
    turned = [roll(o, 64) for o in orig]
    out = []
    for g in range(8):
        m = g // 2
        if g % 2 == 0:
            out.append(orig[m] * low + turned[4 + m] * high)
        else:
            out.append(turned[m] * low + orig[4 + m] * high)
    return out


def from_halves(parts, masks):
    low, high = masks[:2]
    turned = [roll(p, 64) for p in parts]
    first = [parts[2 * m] * low + turned[2 * m + 1] * high for m in range(4)]
    second = [turned[2 * m] * low + parts[2 * m + 1] * high for m in range(4)]
    return first + second


def put_shifts(parts, dst, at, masks):
    low, high, ge2, lt30 = masks
    before = roll(parts[7], 64) * high
    after = roll(parts[0], 64) * low
    for g, t in enumerate([before] + parts + [after]):
        cols = slice(128 * g, 128 * g + 128)
        dst[at, 0:C, cols] = roll(t, 2) * ge2
        dst[at, C : 2 * C, cols] = t
        dst[at, 2 * C : ROWS, cols] = roll(t, 126) * lt30


def split(v):
    return [v[:, 128 * g : 128 * g + 128] for g in range(8)]


def put_zeros(dst, at):
    dst[at] = jnp.zeros((ROWS, WIDE), BF16)


def taps(src, at, start, size):
    return jnp.concatenate(
        [src[at, :, 128 * b + start : 128 * b + start + size] for b in range(3)], axis=0
    )


def outputs_of(e):
    return [(e - 2 * s, s) for s in range(3) if 0 <= e - 2 * s < SLOTS]


def conv_into(acc, w, src):
    seen = set()
    for e in range(SLOTS + 4):
        pairs = outputs_of(e)
        lo, hi = pairs[0][1], pairs[-1][1] + 1
        lhs = w[lo * C : hi * C, :]
        for start in range(0, CELLS, CHUNK):
            y = jnp.dot(lhs, taps(src, e, start, CHUNK), preferred_element_type=F32)
            for p, s in pairs:
                piece = y[(s - lo) * C : (s - lo + 1) * C]
                cols = slice(start, start + CHUNK)
                if (p, start) in seen:
                    acc[p, :, cols] += piece
                else:
                    acc[p, :, cols] = piece
                    seen.add((p, start))


def lane_dot(a, b):
    return lax.dot_general(a, b, (((1,), (1,)), ((), ())), preferred_element_type=F32)


def main_kernel(
    count_ref, x_ref, u_ref, lo_ref, hi_ref, w1_ref, w2_ref, b1_ref,
    hid_ref, head_ref, tail_ref, pay_ref,
    px, pu, ph, w1s, w2s, acc1, acc2, pre, g1, g2,
):
    count = count_ref[0, 0]
    masks = lane_masks()
    for s in range(3):
        w1s[s * C : (s + 1) * C, :] = w1_ref[:, s * TAPS9 : (s + 1) * TAPS9]
    for t in range(27):
        block = w2_ref[:, t * C : (t + 1) * C].astype(F32).T.astype(BF16)
        back = 26 - t
        s, r = back // 9, back % 9
        w2s[s * C : (s + 1) * C, r * C : (r + 1) * C] = block
    for dst in (px, pu):
        put_zeros(dst, SLOTS + 2)
        put_zeros(dst, SLOTS + 3)
    for p in range(SLOTS):
        keep = jnp.where(p < count, 1.0, 0.0).astype(BF16)
        put_shifts(to_halves(x_ref[p] * keep, masks), px, p + 2, masks)
        put_shifts(to_halves(u_ref[p] * keep, masks), pu, p + 2, masks)
    for i in range(2):
        put_shifts(to_halves(lo_ref[i], masks), px, i, masks)
        put_shifts(to_halves(hi_ref[i], masks), px, count + 2 + i, masks)
        put_shifts(to_halves(lo_ref[2 + i], masks), pu, i, masks)
        put_shifts(to_halves(hi_ref[2 + i], masks), pu, count + 2 + i, masks)
    conv_into(acc1, w1s, px)
    conv_into(acc2, w2s, pu)
    bias1 = jnp.zeros((C, CELLS), F32)
    bias2 = jnp.zeros((C, CELLS), F32)
    for p in range(SLOTS):
        keep = jnp.where(p < count, 1.0, 0.0).astype(F32)
        z = acc1[p] + b1_ref[...]
        sig = 1.0 / (1.0 + jnp.exp(-z))
        hid = (z * sig * keep).astype(BF16)
        grad = (acc2[p] * (sig * (1.0 + z * (1.0 - sig))) * keep).astype(BF16)
        hid_ref[p] = hid
        pre[p] = grad
        put_shifts(split(hid), ph, p, masks)
        bias1 += grad.astype(F32)
        bias2 += pu[p + 2, C : 2 * C, 128 : 128 + CELLS].astype(F32) * keep
    for i in range(2):
        head_ref[i] = hid_ref[i]
        tail_ref[i] = hid_ref[count - 2 + i]
    for e in range(SLOTS + 4):
        pairs = outputs_of(e)
        lo, hi = pairs[0][1], pairs[-1][1] + 1
        lhs = jnp.concatenate([pre[p] for p, _ in pairs], axis=0)
        y = lane_dot(lhs, taps(px, e, 0, CELLS))
        if e == 0:
            g1[...] = jnp.zeros((ROWS, TAPS9), F32)
        g1[lo * C : hi * C, :] += y
    for q in range(SLOTS):
        lhs = jnp.concatenate(
            [pu[q + 4 - 2 * s, C : 2 * C, 128 : 128 + CELLS] for s in range(3)], axis=0
        )
        y = lane_dot(lhs, taps(ph, q, 0, CELLS))
        if q == 0:
            g2[...] = y
        else:
            g2[...] += y
    pay_ref[...] = jnp.zeros(pay_ref.shape, BF16)
    pay_ref[0:ROWS, 0:TAPS9] = g1[...].astype(BF16)
    pay_ref[ROWS : 2 * ROWS, 0:TAPS9] = g2[...].astype(BF16)
    pieces = []
    for bias in (bias1, bias2):
        total = jnp.sum(bias, axis=1, keepdims=True)
        high = total.astype(BF16)
        pieces += [high, (total - high.astype(F32)).astype(BF16)]
    pay_ref[0:C, TAPS9 : TAPS9 + 4] = jnp.concatenate(pieces, axis=1)


def spread_kernel(total_ref, g1_ref, g2_ref, bias_ref):
    for s in range(3):
        cols = slice(s * TAPS9, (s + 1) * TAPS9)
        g1_ref[:, cols] = total_ref[s * C : (s + 1) * C, 0:TAPS9].astype(F32)
        g2_ref[:, cols] = total_ref[ROWS + s * C : ROWS + (s + 1) * C, 0:TAPS9].astype(F32)
    four = total_ref[0:C, TAPS9 : TAPS9 + 4].astype(F32)
    bias_ref[...] = jnp.concatenate(
        [four[:, 0:1] + four[:, 1:2], four[:, 2:3] + four[:, 3:4]], axis=1
    )


def out_kernel(count_ref, hid_ref, lo_ref, hi_ref, w2_ref, b2_ref, out_ref, ph, w2s, acc):
    count = count_ref[0, 0]
    masks = lane_masks()
    for s in range(3):
        w2s[s * C : (s + 1) * C, :] = w2_ref[:, s * TAPS9 : (s + 1) * TAPS9]
    put_zeros(ph, SLOTS + 2)
    put_zeros(ph, SLOTS + 3)
    for p in range(SLOTS):
        put_shifts(split(hid_ref[p]), ph, p + 2, masks)
    for i in range(2):
        put_shifts(split(lo_ref[i]), ph, i, masks)
        put_shifts(split(hi_ref[i]), ph, count + 2 + i, masks)
    conv_into(acc, w2s, ph)
    for p in range(SLOTS):
        keep = jnp.where(p < count, 1.0, 0.0).astype(F32)
        z = ((acc[p] + b2_ref[...]) * keep).astype(BF16)
        for g, part in enumerate(from_halves(split(z), masks)):
            out_ref[0, p, :, 128 * g : 128 * g + 128] = part


VM = pl.BlockSpec(memory_space=pltpu.VMEM)
SM = pl.BlockSpec(memory_space=pltpu.SMEM)
PLANES_BF16 = jax.ShapeDtypeStruct((SLOTS, C, CELLS), BF16)
PAIR_BF16 = jax.ShapeDtypeStruct((2, C, CELLS), BF16)
LIMIT = 40 * 1024 * 1024


def run_main(count, x, u, lo, hi, w1, w2, b1, interpret):
    shifted = pltpu.VMEM((SLOTS + 4, ROWS, WIDE), BF16)
    return pl.pallas_call(
        main_kernel,
        out_shape=(
            PLANES_BF16,
            PAIR_BF16,
            PAIR_BF16,
            jax.ShapeDtypeStruct((512, 512), BF16),
        ),
        in_specs=[SM] + [VM] * 7,
        out_specs=[VM] * 4,
        scratch_shapes=[
            shifted,
            shifted,
            pltpu.VMEM((SLOTS, ROWS, WIDE), BF16),
            pltpu.VMEM((ROWS, TAPS9), BF16),
            pltpu.VMEM((ROWS, TAPS9), BF16),
            pltpu.VMEM((SLOTS, C, CELLS), F32),
            pltpu.VMEM((SLOTS, C, CELLS), F32),
            pltpu.VMEM((SLOTS, C, CELLS), BF16),
            pltpu.VMEM((ROWS, TAPS9), F32),
            pltpu.VMEM((ROWS, TAPS9), F32),
        ],
        compiler_params=pltpu.CompilerParams(vmem_limit_bytes=LIMIT),
        cost_estimate=pl.CostEstimate(flops=3_000_000_000, bytes_accessed=4_000_000, transcendentals=500_000),
        interpret=interpret,
        name="grads",
    )(count, x, u, lo, hi, w1, w2, b1)


def run_out(count, hid, lo, hi, w2, b2, interpret):
    return pl.pallas_call(
        out_kernel,
        out_shape=jax.ShapeDtypeStruct((1, SLOTS, C, CELLS), BF16),
        in_specs=[SM] + [VM] * 5,
        out_specs=VM,
        scratch_shapes=[
            pltpu.VMEM((SLOTS + 4, ROWS, WIDE), BF16),
            pltpu.VMEM((ROWS, TAPS9), BF16),
            pltpu.VMEM((SLOTS, C, CELLS), F32),
        ],
        compiler_params=pltpu.CompilerParams(vmem_limit_bytes=LIMIT),
        cost_estimate=pl.CostEstimate(flops=1_000_000_000, bytes_accessed=2_000_000, transcendentals=0),
        interpret=interpret,
        name="decode",
    )(count, hid, lo, hi, w2, b2)


def run_spread(total, interpret):
    grad = jax.ShapeDtypeStruct((C, 27 * C), F32)
    return pl.pallas_call(
        spread_kernel,
        out_shape=(grad, grad, jax.ShapeDtypeStruct((C, 2), F32)),
        in_specs=[VM],
        out_specs=[VM] * 3,
        interpret=interpret,
        name="spread",
    )(total)


def all_reduced(pay, axes):
    parts = lax.axis_size(axes)
    tiles = pay.reshape(64, 8, 4, 128).transpose(0, 2, 1, 3).reshape(parts, -1, 128)
    mine = lax.all_to_all(tiles, axes, 0, 0, tiled=True)
    total = jnp.sum(mine.astype(F32), axis=0, keepdims=True).astype(BF16)
    spread = jnp.broadcast_to(total, (parts,) + total.shape[1:])
    tiles = lax.all_to_all(spread, axes, 0, 0, tiled=True)
    return tiles.reshape(64, 4, 8, 128).transpose(0, 2, 1, 3).reshape(512, 512)


def local(interpret, fields, cotangent, plane_counts, w_first, b_first, w_second, b_second):
    count = plane_counts[0, 0]
    x = fields[0]
    u = cotangent[0]
    size = lax.axis_size("box")
    forward = [(i, i + 1) for i in range(size - 1)]
    backward = [(i + 1, i) for i in range(size - 1)]
    zero = jnp.zeros((), jnp.int32)
    last = lambda v: lax.dynamic_slice(v, (count - 2, zero, zero), (2, C, CELLS))
    lo = lax.ppermute(jnp.concatenate([last(x), last(u)], axis=0), "box", forward)
    hi = lax.ppermute(jnp.concatenate([x[0:2], u[0:2]], axis=0), "box", backward)
    hid, head, tail, pay = run_main(
        plane_counts, x, u, lo, hi, w_first, w_second, b_first[:, None], interpret
    )
    hid_lo = lax.ppermute(tail, "box", forward)
    hid_hi = lax.ppermute(head, "box", backward)
    total = all_reduced(pay, ("box", "snap"))
    decoded = run_out(plane_counts, hid, hid_lo, hid_hi, w_second, b_second[:, None], interpret)
    grad_first, grad_second, bias = run_spread(total, interpret)
    return decoded, grad_first, grad_second, bias[:, 0], bias[:, 1]


def solution(mesh, interpret=False):
    return jax.shard_map(
        functools.partial(local, interpret),
        mesh=mesh,
        in_specs=(
            P("snap", "box", None, None),
            P("snap", "box", None, None),
            P("snap", "box"),
            P(),
            P(),
            P(),
            P(),
        ),
        out_specs=(P("snap", "box", None, None), P(), P(), P(), P()),
        check_vma=False,
    )
```

```python
import functools

import jax
import jax.numpy as jnp
from jax import lax
from jax.experimental import pallas as pl
from jax.experimental.pallas import tpu as pltpu
from jax.sharding import PartitionSpec as P

C = 48
SLOTS = 5
CELLS = 1024
ROWS = 3 * C
TAPS9 = 9 * C
WIDE = CELLS + 256
CHUNK = 256
F32 = jnp.float32
BF16 = jnp.bfloat16


def lane_masks():
    lane = lax.broadcasted_iota(jnp.int32, (C, 128), 1)
    col = lane % 32

    def pick(cond):
        return jnp.where(cond, 1.0, 0.0).astype(BF16)

    return pick(lane < 64), pick(lane >= 64), pick(col >= 2), pick(col < 30)


def roll(v, shift):
    return pltpu.roll(v, shift, 1)


def to_halves(v, masks):
    low, high = masks[:2]
    orig = [v[:, 128 * h : 128 * h + 128] for h in range(8)]
    turned = [roll(o, 64) for o in orig]
    out = []
    for g in range(8):
        m = g // 2
        if g % 2 == 0:
            out.append(orig[m] * low + turned[4 + m] * high)
        else:
            out.append(turned[m] * low + orig[4 + m] * high)
    return out


def from_halves(parts, masks):
    low, high = masks[:2]
    turned = [roll(p, 64) for p in parts]
    first = [parts[2 * m] * low + turned[2 * m + 1] * high for m in range(4)]
    second = [turned[2 * m] * low + parts[2 * m + 1] * high for m in range(4)]
    return first + second


def put_shifts(parts, dst, at, masks):
    low, high, ge2, lt30 = masks
    before = roll(parts[7], 64) * high
    after = roll(parts[0], 64) * low
    for g, t in enumerate([before] + parts + [after]):
        cols = slice(128 * g, 128 * g + 128)
        dst[at, 0:C, cols] = roll(t, 2) * ge2
        dst[at, C : 2 * C, cols] = t
        dst[at, 2 * C : ROWS, cols] = roll(t, 126) * lt30


def split(v):
    return [v[:, 128 * g : 128 * g + 128] for g in range(8)]


def put_zeros(dst, at):
    dst[at] = jnp.zeros((ROWS, WIDE), BF16)


def taps(src, at, start, size):
    return jnp.concatenate(
        [src[at, :, 128 * b + start : 128 * b + start + size] for b in range(3)], axis=0
    )


def outputs_of(q):
    return [(q + 2 - 2 * s, s) for s in range(3) if 0 <= q + 2 - 2 * s < SLOTS]


def conv_local(acc, w, src):
    seen = set()
    for q in range(SLOTS):
        pairs = outputs_of(q)
        lo, hi = pairs[0][1], pairs[-1][1] + 1
        lhs = w[lo * C : hi * C, :]
        for start in range(0, CELLS, CHUNK):
            y = jnp.dot(lhs, taps(src, q, start, CHUNK), preferred_element_type=F32)
            cols = slice(start, start + CHUNK)
            for p, s in pairs:
                piece = y[(s - lo) * C : (s - lo + 1) * C]
                if (p, start) in seen:
                    acc[p, :, cols] += piece
                else:
                    acc[p, :, cols] = piece
                    seen.add((p, start))


def conv_halo(acc, w, src, count):
    for i in range(2):
        for start in range(0, CELLS, CHUNK):
            cols = slice(start, start + CHUNK)
            below = taps(src, i, start, CHUNK)
            acc[i, :, cols] += jnp.dot(w[0:C, :], below, preferred_element_type=F32)
            above = taps(src, 2 + i, start, CHUNK)
            y = jnp.dot(w[2 * C : 3 * C, :], above, preferred_element_type=F32)
            acc[count - 2 + i, :, cols] += y


def lane_dot(a, b):
    return lax.dot_general(a, b, (((1,), (1,)), ((), ())), preferred_element_type=F32)


def middle(ref, at):
    return ref[at, C : 2 * C, 128 : 128 + CELLS]


def stack_taps(w_ref, dst):
    for s in range(3):
        dst[s * C : (s + 1) * C, :] = w_ref[:, s * TAPS9 : (s + 1) * TAPS9]


def front_kernel(count_ref, x_ref, u_ref, w1_ref, w2_ref, px, pu, w2s, acc1, acc2, w1s):
    count = count_ref[0, 0]
    masks = lane_masks()
    stack_taps(w1_ref, w1s)
    turned = w2_ref[...].astype(F32).T
    for s in range(3):
        rows = [26 - 9 * s - r for r in range(9)]
        w2s[s * C : (s + 1) * C, :] = jnp.concatenate(
            [turned[t * C : (t + 1) * C] for t in rows], axis=1
        ).astype(BF16)
    for p in range(SLOTS):
        keep = jnp.where(p < count, 1.0, 0.0).astype(BF16)
        put_shifts(to_halves(x_ref[p] * keep, masks), px, p, masks)
        put_shifts(to_halves(u_ref[p] * keep, masks), pu, p, masks)
    conv_local(acc1, w1s, px)
    conv_local(acc2, w2s, pu)


def main_kernel(
    count_ref, px, pu, w2s, acc1, acc2, lo_ref, hi_ref, w1_ref, b1_ref,
    ph, head_ref, tail_ref, tiles,
    hx, hu, ue, w1s, more1, more2, pre, g1, g2,
):
    count = count_ref[0, 0]
    masks = lane_masks()
    stack_taps(w1_ref, w1s)
    for i in range(2):
        for src, at in ((lo_ref, i), (hi_ref, 2 + i)):
            put_shifts(to_halves(src[i], masks), hx, at, masks)
            put_shifts(to_halves(src[2 + i], masks), hu, at, masks)
    for p in range(SLOTS):
        more1[p] = acc1[p]
        more2[p] = acc2[p]
        ue[p + 2] = middle(pu, p)
    ue[SLOTS + 2] = jnp.zeros((C, CELLS), BF16)
    ue[SLOTS + 3] = jnp.zeros((C, CELLS), BF16)
    for i in range(2):
        ue[i] = middle(hu, i)
        ue[count + 2 + i] = middle(hu, 2 + i)
    conv_halo(more1, w1s, hx, count)
    conv_halo(more2, w2s, hu, count)
    bias1 = jnp.zeros((C, 128), F32)
    bias2 = jnp.zeros((C, 128), F32)
    for p in range(SLOTS):
        keep = jnp.where(p < count, 1.0, 0.0).astype(F32)
        parts = []
        for g in range(8):
            cols = slice(128 * g, 128 * g + 128)
            z = more1[p, :, cols] + b1_ref[...]
            sig = 1.0 / (1.0 + jnp.exp(-z))
            parts.append((z * sig * keep).astype(BF16))
            slope = sig * (1.0 + z * (1.0 - sig))
            grad = (more2[p, :, cols] * slope * keep).astype(BF16)
            pre[p, :, cols] = grad
            bias1 += grad.astype(F32)
            bias2 += pu[p, C : 2 * C, 128 * g + 128 : 128 * g + 256].astype(F32)
        put_shifts(parts, ph, p, masks)
    for i in range(2):
        head_ref[i] = middle(ph, i)
        tail_ref[i] = middle(ph, count - 2 + i)
    for q in range(SLOTS):
        lhs = jnp.concatenate([ue[q + 4 - 2 * s] for s in range(3)], axis=0)
        y = lane_dot(lhs, taps(ph, q, 0, CELLS))
        if q == 0:
            g2[...] = y
        else:
            g2[...] += y
    g1[...] = jnp.zeros((ROWS, TAPS9), F32)
    for q in range(SLOTS):
        pairs = outputs_of(q)
        lo, hi = pairs[0][1], pairs[-1][1] + 1
        lhs = jnp.concatenate([pre[p] for p, _ in pairs], axis=0)
        g1[lo * C : hi * C, :] += lane_dot(lhs, taps(px, q, 0, CELLS))
    for i in range(2):
        g1[0:C, :] += lane_dot(pre[i], taps(hx, i, 0, CELLS))
        g1[2 * C : ROWS, :] += lane_dot(pre[count - 2 + i], taps(hx, 2 + i, 0, CELLS))
    columns = []
    for bias in (bias1, bias2):
        total = jnp.sum(bias, axis=1, keepdims=True)
        high = total.astype(BF16).astype(F32)
        columns += [high, total - high]
    extra = jnp.concatenate(columns + [jnp.zeros((C, 28), F32)], axis=1)
    none = jnp.zeros((16, 32), F32)
    for j in range(9):
        ends = []
        for r in (2 * j, 2 * j + 1):
            src, row = (g1, r * 16) if r < 9 else (g2, r * 16 - ROWS)
            for l in range(3):
                tiles[r * 3 + l] = src[row : row + 16, 128 * l : 128 * l + 128].astype(BF16)
            ends.append(src[row : row + 16, 384:TAPS9])
        ends.append(extra[16 * j : 16 * j + 16] if j < 3 else none)
        tiles[54 + j] = jnp.concatenate(ends, axis=1).astype(BF16)
    tiles[63] = jnp.zeros((16, 128), BF16)


def spread_kernel(tiles, g1_ref, g2_ref, bias1_ref, bias2_ref):
    for r in range(18):
        out = g1_ref if r < 9 else g2_ref
        s, row = (r % 9) // 3, (r % 3) * 16
        parts = [tiles[r * 3 + l].astype(F32) for l in range(3)]
        at = C * (r % 2)
        parts.append(tiles[54 + r // 2].astype(F32)[:, at : at + C])
        out[row : row + 16, s * TAPS9 : (s + 1) * TAPS9] = jnp.concatenate(parts, axis=1)
    four = jnp.concatenate([tiles[54 + j].astype(F32)[:, 96:100] for j in range(3)], axis=0)
    row = lax.broadcasted_iota(jnp.int32, (C, C), 0)
    col = lax.broadcasted_iota(jnp.int32, (C, C), 1)
    for out, j in ((bias1_ref, 0), (bias2_ref, 2)):
        both = four[:, j : j + 1] + four[:, j + 1 : j + 2]
        out[...] = jnp.sum(jnp.where(row == col, both, 0.0), axis=0, keepdims=True)


def out_kernel(count_ref, ph, lo_ref, hi_ref, w2_ref, b2_ref, out_ref, hh, w2s, acc):
    count = count_ref[0, 0]
    masks = lane_masks()
    stack_taps(w2_ref, w2s)
    for i in range(2):
        put_shifts(split(lo_ref[i]), hh, i, masks)
        put_shifts(split(hi_ref[i]), hh, 2 + i, masks)
    conv_local(acc, w2s, ph)
    conv_halo(acc, w2s, hh, count)
    for p in range(SLOTS):
        keep = jnp.where(p < count, 1.0, 0.0).astype(F32)
        z = ((acc[p] + b2_ref[...]) * keep).astype(BF16)
        for g, part in enumerate(from_halves(split(z), masks)):
            out_ref[0, p, :, 128 * g : 128 * g + 128] = part


TILES = 64
VM = pl.BlockSpec(memory_space=pltpu.VMEM)
SM = pl.BlockSpec(memory_space=pltpu.SMEM)
PAIR_BF16 = jax.ShapeDtypeStruct((2, C, CELLS), BF16)
SHIFTED = jax.ShapeDtypeStruct((SLOTS, ROWS, WIDE), BF16)
SUMS = jax.ShapeDtypeStruct((SLOTS, C, CELLS), F32)
WEIGHT = (ROWS, TAPS9)
MIB = 1024 * 1024


def call(kernel, name, args, outs, scratch, limit, flops, interpret):
    return pl.pallas_call(
        kernel,
        out_shape=outs,
        in_specs=[SM if a.dtype == jnp.int32 else VM for a in args],
        out_specs=[VM] * len(outs),
        scratch_shapes=[pltpu.VMEM(shape, kind) for shape, kind in scratch],
        compiler_params=pltpu.CompilerParams(vmem_limit_bytes=limit * MIB),
        cost_estimate=pl.CostEstimate(flops=flops, bytes_accessed=2_000_000, transcendentals=0),
        interpret=interpret,
        name=name,
    )(*args)


def gradient_sum(tiles):
    axes = ("box", "snap")
    parts = lax.axis_size(axes)
    mine = lax.all_to_all(tiles.reshape(parts, -1, 128), axes, 0, 0, tiled=True)
    total = jnp.sum(mine.astype(F32), axis=0, keepdims=True).astype(BF16)
    spread = jnp.broadcast_to(total, (parts,) + total.shape[1:])
    return lax.all_to_all(spread, axes, 0, 0, tiled=True).reshape(TILES, 16, 128)


def local(interpret, fields, cotangent, plane_counts, w_first, b_first, w_second, b_second):
    count = plane_counts[0, 0]
    x = fields[0]
    u = cotangent[0]
    size = lax.axis_size("box")
    forward = [(i, i + 1) for i in range(size - 1)]
    backward = [(i + 1, i) for i in range(size - 1)]
    zero = jnp.zeros((), jnp.int32)
    last = lambda v: lax.dynamic_slice(v, (count - 2, zero, zero), (2, C, CELLS))
    lo = lax.ppermute(jnp.concatenate([last(x), last(u)], axis=0), "box", forward)
    hi = lax.ppermute(jnp.concatenate([x[0:2], u[0:2]], axis=0), "box", backward)
    px, pu, w2s, acc1, acc2 = call(
        front_kernel, "front", (plane_counts, x, u, w_first, w_second),
        (SHIFTED, SHIFTED, jax.ShapeDtypeStruct(WEIGHT, BF16), SUMS, SUMS),
        [(WEIGHT, BF16)], 16, 1_200_000_000, interpret,
    )
    halo = ((4, ROWS, WIDE), BF16)
    ph, head, tail, tiles = call(
        main_kernel, "grads",
        (plane_counts, px, pu, w2s, acc1, acc2, lo, hi, w_first, b_first[:, None]),
        (SHIFTED, PAIR_BF16, PAIR_BF16, jax.ShapeDtypeStruct((TILES, 16, 128), BF16)),
        [
            halo, halo, ((SLOTS + 4, C, CELLS), BF16), (WEIGHT, BF16),
            ((SLOTS, C, CELLS), F32), ((SLOTS, C, CELLS), F32), ((SLOTS, C, CELLS), BF16),
            (WEIGHT, F32), (WEIGHT, F32),
        ],
        32, 2_000_000_000, interpret,
    )
    hid_lo = lax.ppermute(tail, "box", forward)
    hid_hi = lax.ppermute(head, "box", backward)
    tiles = gradient_sum(tiles)
    (decoded,) = call(
        out_kernel, "decode", (plane_counts, ph, hid_lo, hid_hi, w_second, b_second[:, None]),
        (jax.ShapeDtypeStruct((1, SLOTS, C, CELLS), BF16),),
        [halo, (WEIGHT, BF16), ((SLOTS, C, CELLS), F32)], 20, 1_000_000_000, interpret,
    )
    grad = jax.ShapeDtypeStruct((C, 27 * C), F32)
    line = jax.ShapeDtypeStruct((1, C), F32)
    grad_first, grad_second, bias_first, bias_second = call(
        spread_kernel, "spread", (tiles,), (grad, grad, line, line), [], 8, 100_000_000, interpret,
    )
    return decoded, grad_first, grad_second, bias_first[0], bias_second[0]


def solution(mesh, interpret=False):
    return jax.shard_map(
        functools.partial(local, interpret),
        mesh=mesh,
        in_specs=(
            P("snap", "box", None, None),
            P("snap", "box", None, None),
            P("snap", "box"),
            P(),
            P(),
            P(),
            P(),
        ),
        out_specs=(P("snap", "box", None, None), P(), P(), P(), P()),
        check_vma=False,
    )
```

```python
import functools

import jax
import jax.numpy as jnp
from jax import lax
from jax.experimental import pallas as pl
from jax.experimental.pallas import tpu as pltpu
from jax.sharding import PartitionSpec as P

C = 48
SLOTS = 5
CELLS = 1024
ROWS = 3 * C
TAPS9 = 9 * C
WIDE = CELLS + 256
CHUNK = 256
F32 = jnp.float32
BF16 = jnp.bfloat16


def lane_masks():
    lane = lax.broadcasted_iota(jnp.int32, (C, 128), 1)
    col = lane % 32

    def pick(cond):
        return jnp.where(cond, 1.0, 0.0).astype(BF16)

    return pick(lane < 64), pick(lane >= 64), pick(col >= 2), pick(col < 30)


def roll(v, shift):
    return pltpu.roll(v, shift, 1)


def to_halves(v, masks):
    low, high = masks[:2]
    orig = [v[:, 128 * h : 128 * h + 128] for h in range(8)]
    turned = [roll(o, 64) for o in orig]
    out = []
    for g in range(8):
        m = g // 2
        if g % 2 == 0:
            out.append(orig[m] * low + turned[4 + m] * high)
        else:
            out.append(turned[m] * low + orig[4 + m] * high)
    return out


def from_halves(parts, masks):
    low, high = masks[:2]
    turned = [roll(p, 64) for p in parts]
    first = [parts[2 * m] * low + turned[2 * m + 1] * high for m in range(4)]
    second = [turned[2 * m] * low + parts[2 * m + 1] * high for m in range(4)]
    return first + second


def put_shifts(parts, dst, at, masks):
    low, high, ge2, lt30 = masks
    before = roll(parts[7], 64) * high
    after = roll(parts[0], 64) * low
    for g, t in enumerate([before] + parts + [after]):
        cols = slice(128 * g, 128 * g + 128)
        dst[at, 0:C, cols] = roll(t, 2) * ge2
        dst[at, C : 2 * C, cols] = t
        dst[at, 2 * C : ROWS, cols] = roll(t, 126) * lt30


def split(v):
    return [v[:, 128 * g : 128 * g + 128] for g in range(8)]


def put_zeros(dst, at):
    dst[at] = jnp.zeros((ROWS, WIDE), BF16)


def taps(src, at, start, size):
    return jnp.concatenate(
        [src[at, :, 128 * b + start : 128 * b + start + size] for b in range(3)], axis=0
    )


def outputs_of(q):
    return [(q + 2 - 2 * s, s) for s in range(3) if 0 <= q + 2 - 2 * s < SLOTS]


def conv_local(acc, w, src):
    seen = set()
    for q in range(SLOTS):
        pairs = outputs_of(q)
        lo, hi = pairs[0][1], pairs[-1][1] + 1
        lhs = w[lo * C : hi * C, :]
        for start in range(0, CELLS, CHUNK):
            y = jnp.dot(lhs, taps(src, q, start, CHUNK), preferred_element_type=F32)
            cols = slice(start, start + CHUNK)
            for p, s in pairs:
                piece = y[(s - lo) * C : (s - lo + 1) * C]
                if (p, start) in seen:
                    acc[p, :, cols] += piece
                else:
                    acc[p, :, cols] = piece
                    seen.add((p, start))


def conv_halo(acc, w, src, count):
    for i in range(2):
        for start in range(0, CELLS, CHUNK):
            cols = slice(start, start + CHUNK)
            below = taps(src, i, start, CHUNK)
            acc[i, :, cols] += jnp.dot(w[0:C, :], below, preferred_element_type=F32)
            above = taps(src, 2 + i, start, CHUNK)
            y = jnp.dot(w[2 * C : 3 * C, :], above, preferred_element_type=F32)
            acc[count - 2 + i, :, cols] += y


def lane_dot(a, b):
    return lax.dot_general(a, b, (((1,), (1,)), ((), ())), preferred_element_type=F32)


def padded(parts, masks):
    low, high = masks[:2]
    return [roll(parts[7], 64) * high] + parts + [roll(parts[0], 64) * low]


def rows_of(src, planes):
    pieces = [
        src[p, :, 128 * (2 - b) : 128 * (2 - b) + CELLS] for p in planes for b in range(3)
    ]
    return jnp.concatenate(pieces, axis=0)


def center(src, at):
    return src[at, :, 128 : 128 + CELLS]


def middle(ref, at):
    return ref[at, C : 2 * C, 128 : 128 + CELLS]


def stack_taps(w_ref, dst):
    for s in range(3):
        dst[s * C : (s + 1) * C, :] = w_ref[:, s * TAPS9 : (s + 1) * TAPS9]


def front_kernel(count_ref, x_ref, u_ref, w1_ref, w2_ref, px, pu, w2s, acc1, acc2, w1s):
    count = count_ref[0, 0]
    masks = lane_masks()
    stack_taps(w1_ref, w1s)
    turned = w2_ref[...].astype(F32).T
    for s in range(3):
        rows = [26 - 9 * s - r for r in range(9)]
        w2s[s * C : (s + 1) * C, :] = jnp.concatenate(
            [turned[t * C : (t + 1) * C] for t in rows], axis=1
        ).astype(BF16)
    for p in range(SLOTS):
        keep = jnp.where(p < count, 1.0, 0.0).astype(BF16)
        put_shifts(to_halves(x_ref[p] * keep, masks), px, p, masks)
        put_shifts(to_halves(u_ref[p] * keep, masks), pu, p, masks)
    conv_local(acc1, w1s, px)
    conv_local(acc2, w2s, pu)


def main_kernel(
    count_ref, px, pu, w2s, acc1, acc2, lo_ref, hi_ref, w1_ref, b1_ref,
    hid, head_ref, tail_ref, tiles,
    ph, hx, hu, ue, w1s, more1, more2, pre, g1, g2,
):
    count = count_ref[0, 0]
    masks = lane_masks()
    stack_taps(w1_ref, w1s)
    for i in range(2):
        for src, at in ((lo_ref, i), (hi_ref, 2 + i)):
            put_shifts(to_halves(src[i], masks), hx, at, masks)
            put_shifts(to_halves(src[2 + i], masks), hu, at, masks)
    for p in range(SLOTS):
        more1[p] = acc1[p]
        more2[p] = acc2[p]
        ue[p + 2] = pu[p, C : 2 * C, :]
    ue[SLOTS + 2] = jnp.zeros((C, WIDE), BF16)
    ue[SLOTS + 3] = jnp.zeros((C, WIDE), BF16)
    for i in range(2):
        ue[i] = hu[i, C : 2 * C, :]
        ue[count + 2 + i] = hu[2 + i, C : 2 * C, :]
    conv_halo(more1, w1s, hx, count)
    conv_halo(more2, w2s, hu, count)
    bias1 = jnp.zeros((C, 128), F32)
    bias2 = jnp.zeros((C, 128), F32)
    for p in range(SLOTS):
        keep = jnp.where(p < count, 1.0, 0.0).astype(F32)
        parts = []
        grads = []
        for g in range(8):
            cols = slice(128 * g, 128 * g + 128)
            z = more1[p, :, cols] + b1_ref[...]
            sig = 1.0 / (1.0 + jnp.exp(-z))
            parts.append((z * sig * keep).astype(BF16))
            slope = sig * (1.0 + z * (1.0 - sig))
            grad = (more2[p, :, cols] * slope * keep).astype(BF16)
            grads.append(grad)
            bias1 += grad.astype(F32)
            bias2 += pu[p, C : 2 * C, 128 * g + 128 : 128 * g + 256].astype(F32)
        put_shifts(parts, ph, p, masks)
        for g, t in enumerate(padded(grads, masks)):
            pre[p, :, 128 * g : 128 * g + 128] = t
    for p in range(SLOTS):
        hid[p] = middle(ph, p)
    for i in range(2):
        head_ref[i] = middle(ph, i)
        tail_ref[i] = middle(ph, count - 2 + i)
    for q in range(SLOTS):
        y = lane_dot(rows_of(ue, [q + 4, q + 2, q]), center(ph, q))
        if q == 0:
            g2[...] = y
        else:
            g2[...] += y
    g1[...] = jnp.zeros((TAPS9, ROWS), F32)
    for q in range(SLOTS):
        pairs = outputs_of(q)
        lo, hi = pairs[0][1], pairs[-1][1] + 1
        y = lane_dot(rows_of(pre, [p for p, _ in pairs]), center(px, q))
        g1[lo * ROWS : hi * ROWS, :] += y
    for i in range(2):
        g1[0:ROWS, :] += lane_dot(rows_of(pre, [i]), center(hx, i))
        y = lane_dot(rows_of(pre, [count - 2 + i]), center(hx, 2 + i))
        g1[2 * ROWS : TAPS9, :] += y
    columns = []
    for bias in (bias1, bias2):
        total = jnp.sum(bias, axis=1, keepdims=True)
        high = total.astype(BF16).astype(F32)
        columns += [high, total - high]
    ends = []
    for r in range(54):
        src, row = (g1, r * 16) if r < 27 else (g2, r * 16 - TAPS9)
        tiles[r] = src[row : row + 16, 0:128].astype(BF16)
        ends.append(src[row : row + 16, 128:ROWS])
    ends += [jnp.zeros((16, 16), F32)] * 2
    for j in range(7):
        tiles[54 + j] = jnp.concatenate(ends[8 * j : 8 * j + 8], axis=1).astype(BF16)
    four = jnp.concatenate(columns, axis=1)
    row = [four[16 * j : 16 * j + 16] for j in range(3)] + [jnp.zeros((16, 116), F32)]
    tiles[61] = jnp.concatenate(row, axis=1).astype(BF16)
    tiles[62] = jnp.zeros((16, 128), BF16)
    tiles[63] = jnp.zeros((16, 128), BF16)


def spread_kernel(tiles, g1_ref, g2_ref, bias1_ref, bias2_ref):
    for r in range(54):
        out = g1_ref if r < 27 else g2_ref
        n, row = (r % 27) // 3, (r % 3) * 16
        at = 16 * (r % 8)
        end = tiles[54 + r // 8].astype(F32)[:, at : at + 16]
        block = jnp.concatenate([tiles[r].astype(F32), end], axis=1)
        out[row : row + 16, n * ROWS : (n + 1) * ROWS] = block
    last = tiles[61].astype(F32)
    four = jnp.concatenate([last[:, 4 * j : 4 * j + 4] for j in range(3)], axis=0)
    row = lax.broadcasted_iota(jnp.int32, (C, C), 0)
    col = lax.broadcasted_iota(jnp.int32, (C, C), 1)
    for out, j in ((bias1_ref, 0), (bias2_ref, 2)):
        both = four[:, j : j + 1] + four[:, j + 1 : j + 2]
        out[...] = jnp.sum(jnp.where(row == col, both, 0.0), axis=0, keepdims=True)


def out_kernel(count_ref, hid, lo_ref, hi_ref, w2_ref, b2_ref, out_ref, ph, hh, w2s, acc):
    count = count_ref[0, 0]
    masks = lane_masks()
    stack_taps(w2_ref, w2s)
    for i in range(2):
        put_shifts(split(lo_ref[i]), hh, i, masks)
        put_shifts(split(hi_ref[i]), hh, 2 + i, masks)
    for p in range(SLOTS):
        put_shifts(split(hid[p]), ph, p, masks)
    conv_local(acc, w2s, ph)
    conv_halo(acc, w2s, hh, count)
    for p in range(SLOTS):
        keep = jnp.where(p < count, 1.0, 0.0).astype(F32)
        z = ((acc[p] + b2_ref[...]) * keep).astype(BF16)
        for g, part in enumerate(from_halves(split(z), masks)):
            out_ref[0, p, :, 128 * g : 128 * g + 128] = part


TILES = 64
VM = pl.BlockSpec(memory_space=pltpu.VMEM)
SM = pl.BlockSpec(memory_space=pltpu.SMEM)
PAIR_BF16 = jax.ShapeDtypeStruct((2, C, CELLS), BF16)
SHIFTED = jax.ShapeDtypeStruct((SLOTS, ROWS, WIDE), BF16)
SUMS = jax.ShapeDtypeStruct((SLOTS, C, CELLS), F32)
WEIGHT = (ROWS, TAPS9)
MIB = 1024 * 1024


def call(kernel, name, args, outs, scratch, limit, flops, interpret):
    return pl.pallas_call(
        kernel,
        out_shape=outs,
        in_specs=[SM if a.dtype == jnp.int32 else VM for a in args],
        out_specs=[VM] * len(outs),
        scratch_shapes=[pltpu.VMEM(shape, kind) for shape, kind in scratch],
        compiler_params=pltpu.CompilerParams(vmem_limit_bytes=limit * MIB),
        cost_estimate=pl.CostEstimate(flops=flops, bytes_accessed=2_000_000, transcendentals=0),
        interpret=interpret,
        name=name,
    )(*args)


def gradient_sum(tiles):
    axes = ("box", "snap")
    parts = lax.axis_size(axes)
    mine = lax.all_to_all(tiles.reshape(parts, -1, 128), axes, 0, 0, tiled=True)
    total = jnp.sum(mine.astype(F32), axis=0, keepdims=True).astype(BF16)
    spread = jnp.broadcast_to(total, (parts,) + total.shape[1:])
    return lax.all_to_all(spread, axes, 0, 0, tiled=True).reshape(TILES, 16, 128)


def local(interpret, fields, cotangent, plane_counts, w_first, b_first, w_second, b_second):
    count = plane_counts[0, 0]
    x = fields[0]
    u = cotangent[0]
    size = lax.axis_size("box")
    forward = [(i, i + 1) for i in range(size - 1)]
    backward = [(i + 1, i) for i in range(size - 1)]
    zero = jnp.zeros((), jnp.int32)
    last = lambda v: lax.dynamic_slice(v, (count - 2, zero, zero), (2, C, CELLS))
    lo = lax.ppermute(jnp.concatenate([last(x), last(u)], axis=0), "box", forward)
    hi = lax.ppermute(jnp.concatenate([x[0:2], u[0:2]], axis=0), "box", backward)
    px, pu, w2s, acc1, acc2 = call(
        front_kernel, "front", (plane_counts, x, u, w_first, w_second),
        (SHIFTED, SHIFTED, jax.ShapeDtypeStruct(WEIGHT, BF16), SUMS, SUMS),
        [(WEIGHT, BF16)], 16, 1_200_000_000, interpret,
    )
    halo = ((4, ROWS, WIDE), BF16)
    hid, head, tail, tiles = call(
        main_kernel, "grads",
        (plane_counts, px, pu, w2s, acc1, acc2, lo, hi, w_first, b_first[:, None]),
        (jax.ShapeDtypeStruct((SLOTS, C, CELLS), BF16), PAIR_BF16, PAIR_BF16, jax.ShapeDtypeStruct((TILES, 16, 128), BF16)),
        [
            ((SLOTS, ROWS, WIDE), BF16), halo, halo, ((SLOTS + 4, C, WIDE), BF16), (WEIGHT, BF16),
            ((SLOTS, C, CELLS), F32), ((SLOTS, C, CELLS), F32), ((SLOTS, C, WIDE), BF16),
            ((TAPS9, ROWS), F32), ((TAPS9, ROWS), F32),
        ],
        32, 2_000_000_000, interpret,
    )
    hid_lo = lax.ppermute(tail, "box", forward)
    hid_hi = lax.ppermute(head, "box", backward)
    tiles = gradient_sum(tiles)
    (decoded,) = call(
        out_kernel, "decode", (plane_counts, hid, hid_lo, hid_hi, w_second, b_second[:, None]),
        (jax.ShapeDtypeStruct((1, SLOTS, C, CELLS), BF16),),
        [((SLOTS, ROWS, WIDE), BF16), halo, (WEIGHT, BF16), ((SLOTS, C, CELLS), F32)], 24, 1_000_000_000, interpret,
    )
    grad = jax.ShapeDtypeStruct((C, 27 * C), F32)
    line = jax.ShapeDtypeStruct((1, C), F32)
    grad_first, grad_second, bias_first, bias_second = call(
        spread_kernel, "spread", (tiles,), (grad, grad, line, line), [], 8, 100_000_000, interpret,
    )
    return decoded, grad_first, grad_second, bias_first[0], bias_second[0]


def solution(mesh, interpret=False):
    return jax.shard_map(
        functools.partial(local, interpret),
        mesh=mesh,
        in_specs=(
            P("snap", "box", None, None),
            P("snap", "box", None, None),
            P("snap", "box"),
            P(),
            P(),
            P(),
            P(),
        ),
        out_specs=(P("snap", "box", None, None), P(), P(), P(), P()),
        check_vma=False,
    )
```

```python
import functools

import jax
import jax.numpy as jnp
from jax import lax
from jax.experimental import pallas as pl
from jax.experimental.pallas import tpu as pltpu
from jax.sharding import PartitionSpec as P

C = 48
SLOTS = 5
CELLS = 1024
ROWS = 3 * C
TAPS9 = 9 * C
WIDE = CELLS + 256
CHUNK = 256
F32 = jnp.float32
BF16 = jnp.bfloat16


def lane_masks():
    lane = lax.broadcasted_iota(jnp.int32, (C, 128), 1)
    col = lane % 32

    def pick(cond):
        return jnp.where(cond, 1.0, 0.0).astype(BF16)

    return pick(lane < 64), pick(lane >= 64), pick(col >= 2), pick(col < 30)


def roll(v, shift):
    return pltpu.roll(v, shift, 1)


def to_halves(v, masks):
    low, high = masks[:2]
    orig = [v[:, 128 * h : 128 * h + 128] for h in range(8)]
    turned = [roll(o, 64) for o in orig]
    out = []
    for g in range(8):
        m = g // 2
        if g % 2 == 0:
            out.append(orig[m] * low + turned[4 + m] * high)
        else:
            out.append(turned[m] * low + orig[4 + m] * high)
    return out


def from_halves(parts, masks):
    low, high = masks[:2]
    turned = [roll(p, 64) for p in parts]
    first = [parts[2 * m] * low + turned[2 * m + 1] * high for m in range(4)]
    second = [turned[2 * m] * low + parts[2 * m + 1] * high for m in range(4)]
    return first + second


def put_shifts(parts, dst, at, masks):
    low, high, ge2, lt30 = masks
    before = roll(parts[7], 64) * high
    after = roll(parts[0], 64) * low
    for g, t in enumerate([before] + parts + [after]):
        cols = slice(128 * g, 128 * g + 128)
        dst[at, 0:C, cols] = roll(t, 2) * ge2
        dst[at, C : 2 * C, cols] = t
        dst[at, 2 * C : ROWS, cols] = roll(t, 126) * lt30


def split(v):
    return [v[:, 128 * g : 128 * g + 128] for g in range(8)]


def put_zeros(dst, at):
    dst[at] = jnp.zeros((ROWS, WIDE), BF16)


def taps(src, at, start, size):
    return jnp.concatenate(
        [src[at, :, 128 * b + start : 128 * b + start + size] for b in range(3)], axis=0
    )


def outputs_of(q):
    return [(q + 2 - 2 * s, s) for s in range(3) if 0 <= q + 2 - 2 * s < SLOTS]


def conv_local(acc, w, src):
    seen = set()
    for q in range(SLOTS):
        pairs = outputs_of(q)
        lo, hi = pairs[0][1], pairs[-1][1] + 1
        lhs = w[lo * C : hi * C, :]
        for start in range(0, CELLS, CHUNK):
            y = jnp.dot(lhs, taps(src, q, start, CHUNK), preferred_element_type=F32)
            cols = slice(start, start + CHUNK)
            for p, s in pairs:
                piece = y[(s - lo) * C : (s - lo + 1) * C]
                if (p, start) in seen:
                    acc[p, :, cols] += piece
                else:
                    acc[p, :, cols] = piece
                    seen.add((p, start))


def conv_halo(acc, w, src, first):
    for i in range(2):
        for start in range(0, CELLS, CHUNK):
            cols = slice(start, start + CHUNK)
            y = jnp.dot(w, taps(src, i, start, CHUNK), preferred_element_type=F32)
            acc[first + i, :, cols] += y


def lane_dot(a, b):
    return lax.dot_general(a, b, (((1,), (1,)), ((), ())), preferred_element_type=F32)


def padded(parts, masks):
    low, high = masks[:2]
    return [roll(parts[7], 64) * high] + parts + [roll(parts[0], 64) * low]


def rows_of(src, planes):
    pieces = [
        src[p, :, 128 * (2 - b) : 128 * (2 - b) + CELLS] for p in planes for b in range(3)
    ]
    return jnp.concatenate(pieces, axis=0)


def center(src, at):
    return src[at, :, 128 : 128 + CELLS]


def middle(ref, at):
    return ref[at, C : 2 * C, 128 : 128 + CELLS]


def stack_taps(w_ref, dst):
    for s in range(3):
        dst[s * C : (s + 1) * C, :] = w_ref[:, s * TAPS9 : (s + 1) * TAPS9]


def front_kernel(count_ref, x_ref, u_ref, w1_ref, w2_ref, px, pu, w1s, w2s, acc1, acc2):
    count = count_ref[0, 0]
    masks = lane_masks()
    stack_taps(w1_ref, w1s)
    turned = w2_ref[...].astype(F32).T
    for s in range(3):
        rows = [26 - 9 * s - r for r in range(9)]
        w2s[s * C : (s + 1) * C, :] = jnp.concatenate(
            [turned[t * C : (t + 1) * C] for t in rows], axis=1
        ).astype(BF16)
    for p in range(SLOTS):
        keep = jnp.where(p < count, 1.0, 0.0).astype(BF16)
        put_shifts(to_halves(x_ref[p] * keep, masks), px, p, masks)
        put_shifts(to_halves(u_ref[p] * keep, masks), pu, p, masks)
    conv_local(acc1, w1s, px)
    conv_local(acc2, w2s, pu)


def low_kernel(w1s, w2s, acc1, acc2, lo_ref, lx, lu, sum1, sum2):
    masks = lane_masks()
    for i in range(2):
        put_shifts(to_halves(lo_ref[i], masks), lx, i, masks)
        put_shifts(to_halves(lo_ref[2 + i], masks), lu, i, masks)
    for i in range(2):
        sum1[i] = acc1[i]
        sum2[i] = acc2[i]
    conv_halo(sum1, w1s[0:C, :], lx, 0)
    conv_halo(sum2, w2s[0:C, :], lu, 0)


def main_kernel(
    count_ref, px, pu, w1s, w2s, acc1, acc2, two1, two2, lx, lu, hi_ref, b1_ref,
    hid, head_ref, tail_ref, tiles,
    more1, more2, ph, hx, hu, ue, pre, g1, g2,
):
    count = count_ref[0, 0]
    masks = lane_masks()
    for i in range(2):
        put_shifts(to_halves(hi_ref[i], masks), hx, i, masks)
        put_shifts(to_halves(hi_ref[2 + i], masks), hu, i, masks)
    for p in range(SLOTS):
        ue[p + 2] = pu[p, C : 2 * C, :]
    ue[SLOTS + 2] = jnp.zeros((C, WIDE), BF16)
    ue[SLOTS + 3] = jnp.zeros((C, WIDE), BF16)
    for i in range(2):
        ue[i] = lu[i, C : 2 * C, :]
        ue[count + 2 + i] = hu[i, C : 2 * C, :]
    for p in range(SLOTS):
        more1[p] = two1[p] if p < 2 else acc1[p]
        more2[p] = two2[p] if p < 2 else acc2[p]
    conv_halo(more1, w1s[2 * C : 3 * C, :], hx, count - 2)
    conv_halo(more2, w2s[2 * C : 3 * C, :], hu, count - 2)
    bias1 = jnp.zeros((C, 128), F32)
    bias2 = jnp.zeros((C, 128), F32)
    for p in range(SLOTS):
        keep = jnp.where(p < count, 1.0, 0.0).astype(F32)
        parts = []
        grads = []
        for g in range(8):
            cols = slice(128 * g, 128 * g + 128)
            z = more1[p, :, cols] + b1_ref[...]
            sig = 1.0 / (1.0 + jnp.exp(-z))
            parts.append((z * sig * keep).astype(BF16))
            slope = sig * (1.0 + z * (1.0 - sig))
            grad = (more2[p, :, cols] * slope * keep).astype(BF16)
            grads.append(grad)
            bias1 += grad.astype(F32)
            bias2 += pu[p, C : 2 * C, 128 * g + 128 : 128 * g + 256].astype(F32)
        put_shifts(parts, ph, p, masks)
        for g, t in enumerate(padded(grads, masks)):
            pre[p, :, 128 * g : 128 * g + 128] = t
    for p in range(SLOTS):
        hid[p] = middle(ph, p)
    for i in range(2):
        head_ref[i] = middle(ph, i)
        tail_ref[i] = middle(ph, count - 2 + i)
    for q in range(SLOTS):
        y = lane_dot(rows_of(ue, [q + 4, q + 2, q]), center(ph, q))
        if q == 0:
            g2[...] = y
        else:
            g2[...] += y
    g1[...] = jnp.zeros((TAPS9, ROWS), F32)
    for q in range(SLOTS):
        pairs = outputs_of(q)
        lo, hi = pairs[0][1], pairs[-1][1] + 1
        y = lane_dot(rows_of(pre, [p for p, _ in pairs]), center(px, q))
        g1[lo * ROWS : hi * ROWS, :] += y
    for i in range(2):
        g1[0:ROWS, :] += lane_dot(rows_of(pre, [i]), center(lx, i))
        y = lane_dot(rows_of(pre, [count - 2 + i]), center(hx, i))
        g1[2 * ROWS : TAPS9, :] += y
    columns = []
    for bias in (bias1, bias2):
        total = jnp.sum(bias, axis=1, keepdims=True)
        high = total.astype(BF16).astype(F32)
        columns += [high, total - high]
    ends = []
    for r in range(54):
        src, row = (g1, r * 16) if r < 27 else (g2, r * 16 - TAPS9)
        tiles[r] = src[row : row + 16, 0:128].astype(BF16)
        ends.append(src[row : row + 16, 128:ROWS].astype(BF16))
    ends += [jnp.zeros((16, 16), BF16)] * 2
    for j in range(7):
        tiles[54 + j] = jnp.concatenate(ends[8 * j : 8 * j + 8], axis=1)
    four = jnp.concatenate(columns, axis=1)
    row = [four[16 * j : 16 * j + 16] for j in range(3)] + [jnp.zeros((16, 116), F32)]
    tiles[61] = jnp.concatenate(row, axis=1).astype(BF16)
    tiles[62] = jnp.zeros((16, 128), BF16)
    tiles[63] = jnp.zeros((16, 128), BF16)


def spread_kernel(tiles, g1_ref, g2_ref, bias1_ref, bias2_ref):
    for r in range(6):
        pieces = []
        for n in range(9):
            t = (r // 3) * 27 + n * 3 + r % 3
            pieces += [tiles[t], tiles[54 + t // 8, :, 16 * (t % 8) : 16 * (t % 8) + 16]]
        out = g1_ref if r < 3 else g2_ref
        row = (r % 3) * 16
        out[row : row + 16, :] = jnp.concatenate(pieces, axis=1).astype(F32)
    last = tiles[61].astype(F32)
    four = jnp.concatenate([last[:, 4 * j : 4 * j + 4] for j in range(3)], axis=0)
    row = lax.broadcasted_iota(jnp.int32, (C, C), 0)
    col = lax.broadcasted_iota(jnp.int32, (C, C), 1)
    for out, j in ((bias1_ref, 0), (bias2_ref, 2)):
        both = four[:, j : j + 1] + four[:, j + 1 : j + 2]
        out[...] = jnp.sum(jnp.where(row == col, both, 0.0), axis=0, keepdims=True)


def out_kernel(count_ref, hid, lo_ref, hi_ref, w2_ref, b2_ref, out_ref, ph, lh, hh, w2s, acc):
    count = count_ref[0, 0]
    masks = lane_masks()
    stack_taps(w2_ref, w2s)
    for i in range(2):
        put_shifts(split(lo_ref[i]), lh, i, masks)
        put_shifts(split(hi_ref[i]), hh, i, masks)
    for p in range(SLOTS):
        put_shifts(split(hid[p]), ph, p, masks)
    conv_local(acc, w2s, ph)
    conv_halo(acc, w2s[0:C, :], lh, 0)
    conv_halo(acc, w2s[2 * C : 3 * C, :], hh, count - 2)
    for p in range(SLOTS):
        keep = jnp.where(p < count, 1.0, 0.0).astype(F32)
        z = ((acc[p] + b2_ref[...]) * keep).astype(BF16)
        for g, part in enumerate(from_halves(split(z), masks)):
            out_ref[0, p, :, 128 * g : 128 * g + 128] = part


TILES = 64
VM = pl.BlockSpec(memory_space=pltpu.VMEM)
SM = pl.BlockSpec(memory_space=pltpu.SMEM)
PAIR_BF16 = jax.ShapeDtypeStruct((2, C, CELLS), BF16)
SHIFTED = jax.ShapeDtypeStruct((SLOTS, ROWS, WIDE), BF16)
SUMS = jax.ShapeDtypeStruct((SLOTS, C, CELLS), F32)
WEIGHT = (ROWS, TAPS9)
MIB = 1024 * 1024


def call(kernel, name, args, outs, scratch, limit, flops, interpret):
    return pl.pallas_call(
        kernel,
        out_shape=outs,
        in_specs=[SM if a.dtype == jnp.int32 else VM for a in args],
        out_specs=[VM] * len(outs),
        scratch_shapes=[pltpu.VMEM(shape, kind) for shape, kind in scratch],
        compiler_params=pltpu.CompilerParams(vmem_limit_bytes=limit * MIB),
        cost_estimate=pl.CostEstimate(flops=flops, bytes_accessed=2_000_000, transcendentals=0),
        interpret=interpret,
        name=name,
    )(*args)


def gradient_sum(tiles):
    axes = ("box", "snap")
    parts = lax.axis_size(axes)
    mine = lax.all_to_all(tiles.reshape(parts, -1, 128), axes, 0, 0, tiled=True)
    total = jnp.sum(mine.astype(F32), axis=0, keepdims=True).astype(BF16)
    spread = jnp.broadcast_to(total, (parts,) + total.shape[1:])
    return lax.all_to_all(spread, axes, 0, 0, tiled=True).reshape(TILES, 16, 128)


def local(interpret, fields, cotangent, plane_counts, w_first, b_first, w_second, b_second):
    count = plane_counts[0, 0]
    x = fields[0]
    u = cotangent[0]
    size = lax.axis_size("box")
    forward = [(i, i + 1) for i in range(size - 1)]
    backward = [(i + 1, i) for i in range(size - 1)]
    zero = jnp.zeros((), jnp.int32)
    last = lambda v: lax.dynamic_slice(v, (count - 2, zero, zero), (2, C, CELLS))
    lo = lax.ppermute(jnp.concatenate([last(x), last(u)], axis=0), "box", forward)
    hi = lax.ppermute(jnp.concatenate([x[0:2], u[0:2]], axis=0), "box", backward)
    stacked = jax.ShapeDtypeStruct(WEIGHT, BF16)
    px, pu, w1s, w2s, acc1, acc2 = call(
        front_kernel, "front", (plane_counts, x, u, w_first, w_second),
        (SHIFTED, SHIFTED, stacked, stacked, SUMS, SUMS), [], 16, 1_200_000_000, interpret,
    )
    halo = ((2, ROWS, WIDE), BF16)
    low_shape = jax.ShapeDtypeStruct((2, ROWS, WIDE), BF16)
    two = jax.ShapeDtypeStruct((2, C, CELLS), F32)
    lx, lu, two1, two2 = call(
        low_kernel, "low", (w1s, w2s, acc1, acc2, lo),
        (low_shape, low_shape, two, two), [], 16, 300_000_000, interpret,
    )
    hid, head, tail, tiles = call(
        main_kernel, "grads",
        (plane_counts, px, pu, w1s, w2s, acc1, acc2, two1, two2, lx, lu, hi, b_first[:, None]),
        (jax.ShapeDtypeStruct((SLOTS, C, CELLS), BF16), PAIR_BF16, PAIR_BF16, jax.ShapeDtypeStruct((TILES, 16, 128), BF16)),
        [
            ((SLOTS, C, CELLS), F32), ((SLOTS, C, CELLS), F32), ((SLOTS, ROWS, WIDE), BF16),
            halo, halo, ((SLOTS + 4, C, WIDE), BF16), ((SLOTS, C, WIDE), BF16),
            ((TAPS9, ROWS), F32), ((TAPS9, ROWS), F32),
        ],
        32, 2_000_000_000, interpret,
    )
    hid_lo = lax.ppermute(tail, "box", forward)
    hid_hi = lax.ppermute(head, "box", backward)
    tiles = gradient_sum(tiles)
    (decoded,) = call(
        out_kernel, "decode", (plane_counts, hid, hid_lo, hid_hi, w_second, b_second[:, None]),
        (jax.ShapeDtypeStruct((1, SLOTS, C, CELLS), BF16),),
        [((SLOTS, ROWS, WIDE), BF16), halo, halo, (WEIGHT, BF16), ((SLOTS, C, CELLS), F32)], 24, 1_000_000_000, interpret,
    )
    grad = jax.ShapeDtypeStruct((C, 27 * C), F32)
    line = jax.ShapeDtypeStruct((1, C), F32)
    grad_first, grad_second, bias_first, bias_second = call(
        spread_kernel, "spread", (tiles,), (grad, grad, line, line), [], 8, 100_000_000, interpret,
    )
    return decoded, grad_first, grad_second, bias_first[0], bias_second[0]


def solution(mesh, interpret=False):
    return jax.shard_map(
        functools.partial(local, interpret),
        mesh=mesh,
        in_specs=(
            P("snap", "box", None, None),
            P("snap", "box", None, None),
            P("snap", "box"),
            P(),
            P(),
            P(),
            P(),
        ),
        out_specs=(P("snap", "box", None, None), P(), P(), P(), P()),
        check_vma=False,
    )
```

```python
import functools

import jax
import jax.numpy as jnp
from jax import lax
from jax.experimental import pallas as pl
from jax.experimental.pallas import tpu as pltpu
from jax.sharding import PartitionSpec as P

C = 48
SLOTS = 5
CELLS = 1024
ROWS = 3 * C
TAPS9 = 9 * C
WIDE = CELLS + 256
CHUNK = 256
F32 = jnp.float32
BF16 = jnp.bfloat16


def lane_masks():
    lane = lax.broadcasted_iota(jnp.int32, (C, 128), 1)
    col = lane % 32

    def pick(cond):
        return jnp.where(cond, 1.0, 0.0).astype(BF16)

    return pick(lane < 64), pick(lane >= 64), pick(col >= 2), pick(col < 30)


def roll(v, shift):
    return pltpu.roll(v, shift, 1)


def to_halves(v, masks):
    low, high = masks[:2]
    orig = [v[:, 128 * h : 128 * h + 128] for h in range(8)]
    turned = [roll(o, 64) for o in orig]
    out = []
    for g in range(8):
        m = g // 2
        if g % 2 == 0:
            out.append(orig[m] * low + turned[4 + m] * high)
        else:
            out.append(turned[m] * low + orig[4 + m] * high)
    return out


def from_halves(parts, masks):
    low, high = masks[:2]
    turned = [roll(p, 64) for p in parts]
    first = [parts[2 * m] * low + turned[2 * m + 1] * high for m in range(4)]
    second = [turned[2 * m] * low + parts[2 * m + 1] * high for m in range(4)]
    return first + second


def put_shifts(parts, dst, at, masks):
    low, high, ge2, lt30 = masks
    before = roll(parts[7], 64) * high
    after = roll(parts[0], 64) * low
    for g, t in enumerate([before] + parts + [after]):
        cols = slice(128 * g, 128 * g + 128)
        dst[at, 0:C, cols] = roll(t, 2) * ge2
        dst[at, C : 2 * C, cols] = t
        dst[at, 2 * C : ROWS, cols] = roll(t, 126) * lt30


def split(v):
    return [v[:, 128 * g : 128 * g + 128] for g in range(8)]


def put_zeros(dst, at):
    dst[at] = jnp.zeros((ROWS, WIDE), BF16)


def taps(src, at, start, size):
    return jnp.concatenate(
        [src[at, :, 128 * b + start : 128 * b + start + size] for b in range(3)], axis=0
    )


def outputs_of(q):
    return [(q + 2 - 2 * s, s) for s in range(3) if 0 <= q + 2 - 2 * s < SLOTS]


def conv_local(acc, w, src):
    seen = set()
    for q in range(SLOTS):
        pairs = outputs_of(q)
        lo, hi = pairs[0][1], pairs[-1][1] + 1
        lhs = w[lo * C : hi * C, :]
        for start in range(0, CELLS, CHUNK):
            y = jnp.dot(lhs, taps(src, q, start, CHUNK), preferred_element_type=F32)
            cols = slice(start, start + CHUNK)
            for p, s in pairs:
                piece = y[(s - lo) * C : (s - lo + 1) * C]
                if (p, start) in seen:
                    acc[p, :, cols] += piece
                else:
                    acc[p, :, cols] = piece
                    seen.add((p, start))


def conv_halo(acc, w, src, first):
    for i in range(2):
        for start in range(0, CELLS, CHUNK):
            cols = slice(start, start + CHUNK)
            y = jnp.dot(w, taps(src, i, start, CHUNK), preferred_element_type=F32)
            acc[first + i, :, cols] += y


def lane_dot(a, b):
    return lax.dot_general(a, b, (((1,), (1,)), ((), ())), preferred_element_type=F32)


def padded(parts, masks):
    low, high = masks[:2]
    return [roll(parts[7], 64) * high] + parts + [roll(parts[0], 64) * low]


def rows_of(src, planes):
    pieces = [
        src[p, :, 128 * (2 - b) : 128 * (2 - b) + CELLS] for p in planes for b in range(3)
    ]
    return jnp.concatenate(pieces, axis=0)


def center(src, at):
    return src[at, :, 128 : 128 + CELLS]


def middle(ref, at):
    return ref[at, C : 2 * C, 128 : 128 + CELLS]


def stack_taps(w_ref, dst):
    for s in range(3):
        dst[s * C : (s + 1) * C, :] = w_ref[:, s * TAPS9 : (s + 1) * TAPS9]


def front_kernel(count_ref, x_ref, u_ref, w1_ref, w2_ref, px, pu, w1s, w2s, acc1, acc2):
    count = count_ref[0, 0]
    masks = lane_masks()
    stack_taps(w1_ref, w1s)
    turned = w2_ref[...].astype(F32).T
    for s in range(3):
        rows = [26 - 9 * s - r for r in range(9)]
        w2s[s * C : (s + 1) * C, :] = jnp.concatenate(
            [turned[t * C : (t + 1) * C] for t in rows], axis=1
        ).astype(BF16)
    for p in range(SLOTS):
        keep = jnp.where(p < count, 1.0, 0.0).astype(BF16)
        put_shifts(to_halves(x_ref[p] * keep, masks), px, p, masks)
        put_shifts(to_halves(u_ref[p] * keep, masks), pu, p, masks)
    conv_local(acc1, w1s, px)
    conv_local(acc2, w2s, pu)


def low_kernel(w1s, w2s, acc1, acc2, lo_ref, lx, lu, sum1, sum2):
    masks = lane_masks()
    for i in range(2):
        put_shifts(to_halves(lo_ref[i], masks), lx, i, masks)
        put_shifts(to_halves(lo_ref[2 + i], masks), lu, i, masks)
    for i in range(2):
        sum1[i] = acc1[i]
        sum2[i] = acc2[i]
    conv_halo(sum1, w1s[0:C, :], lx, 0)
    conv_halo(sum2, w2s[0:C, :], lu, 0)


def main_kernel(
    count_ref, px, pu, w1s, w2s, acc1, acc2, two1, two2, lx, lu, hi_ref, b1_ref,
    hid, head_ref, tail_ref, tiles,
    more1, more2, ph, hx, hu, ue, pre, g1, g2,
):
    count = count_ref[0, 0]
    masks = lane_masks()
    for i in range(2):
        put_shifts(to_halves(hi_ref[i], masks), hx, i, masks)
        put_shifts(to_halves(hi_ref[2 + i], masks), hu, i, masks)
    for p in range(SLOTS):
        ue[p + 2] = pu[p, C : 2 * C, :]
    ue[SLOTS + 2] = jnp.zeros((C, WIDE), BF16)
    ue[SLOTS + 3] = jnp.zeros((C, WIDE), BF16)
    for i in range(2):
        ue[i] = lu[i, C : 2 * C, :]
        ue[count + 2 + i] = hu[i, C : 2 * C, :]
    for p in range(SLOTS):
        more1[p] = two1[p] if p < 2 else acc1[p]
        more2[p] = two2[p] if p < 2 else acc2[p]
    conv_halo(more1, w1s[2 * C : 3 * C, :], hx, count - 2)
    conv_halo(more2, w2s[2 * C : 3 * C, :], hu, count - 2)
    bias1 = jnp.zeros((C, 128), F32)
    bias2 = jnp.zeros((C, 128), F32)
    for p in range(SLOTS):
        keep = jnp.where(p < count, 1.0, 0.0).astype(F32)
        parts = []
        grads = []
        for g in range(8):
            cols = slice(128 * g, 128 * g + 128)
            z = more1[p, :, cols] + b1_ref[...]
            sig = 1.0 / (1.0 + jnp.exp(-z))
            parts.append((z * sig * keep).astype(BF16))
            slope = sig * (1.0 + z * (1.0 - sig))
            grad = (more2[p, :, cols] * slope * keep).astype(BF16)
            grads.append(grad)
            bias1 += grad.astype(F32)
            bias2 += pu[p, C : 2 * C, 128 * g + 128 : 128 * g + 256].astype(F32)
        put_shifts(parts, ph, p, masks)
        for g, t in enumerate(padded(grads, masks)):
            pre[p, :, 128 * g : 128 * g + 128] = t
    for p in range(SLOTS):
        hid[p] = middle(ph, p)
    for i in range(2):
        head_ref[i] = middle(ph, i)
        tail_ref[i] = middle(ph, count - 2 + i)
    for q in range(SLOTS):
        y = lane_dot(rows_of(ue, [q + 4, q + 2, q]), center(ph, q))
        if q == 0:
            g2[...] = y
        else:
            g2[...] += y
    g1[...] = jnp.zeros((TAPS9, ROWS), F32)
    for q in range(SLOTS):
        pairs = outputs_of(q)
        lo, hi = pairs[0][1], pairs[-1][1] + 1
        y = lane_dot(rows_of(pre, [p for p, _ in pairs]), center(px, q))
        g1[lo * ROWS : hi * ROWS, :] += y
    for i in range(2):
        g1[0:ROWS, :] += lane_dot(rows_of(pre, [i]), center(lx, i))
        y = lane_dot(rows_of(pre, [count - 2 + i]), center(hx, i))
        g1[2 * ROWS : TAPS9, :] += y
    columns = []
    for bias in (bias1, bias2):
        total = jnp.sum(bias, axis=1, keepdims=True)
        high = total.astype(BF16).astype(F32)
        columns += [high, total - high]
    ends = []
    for r in range(54):
        src, row = (g1, r * 16) if r < 27 else (g2, r * 16 - TAPS9)
        tiles[r] = src[row : row + 16, 0:128].astype(BF16)
        ends.append(src[row : row + 16, 128:ROWS].astype(BF16))
    ends += [jnp.zeros((16, 16), BF16)] * 2
    for j in range(7):
        tiles[54 + j] = jnp.concatenate(ends[8 * j : 8 * j + 8], axis=1)
    four = jnp.concatenate(columns, axis=1)
    row = [four[16 * j : 16 * j + 16] for j in range(3)] + [jnp.zeros((16, 116), F32)]
    tiles[61] = jnp.concatenate(row, axis=1).astype(BF16)
    tiles[62] = jnp.zeros((16, 128), BF16)
    tiles[63] = jnp.zeros((16, 128), BF16)


def total_kernel(rows, src, out):
    total = src[0].astype(F32)
    for i in range(1, src.shape[0]):
        total += src[i].astype(F32)
    copies = total.shape[0] // rows
    part = total[0:rows]
    for i in range(1, copies):
        part += total[i * rows : (i + 1) * rows]
    block = jnp.concatenate([part] * copies, axis=0).astype(BF16)
    for i in range(out.shape[0]):
        out[i] = block


def spread_kernel(tiles, g1_ref, g2_ref, bias1_ref, bias2_ref):
    for r in range(6):
        pieces = []
        for n in range(9):
            t = (r // 3) * 27 + n * 3 + r % 3
            pieces += [tiles[t], tiles[54 + t // 8, :, 16 * (t % 8) : 16 * (t % 8) + 16]]
        out = g1_ref if r < 3 else g2_ref
        row = (r % 3) * 16
        out[row : row + 16, :] = jnp.concatenate(pieces, axis=1).astype(F32)
    last = tiles[61].astype(F32)
    four = jnp.concatenate([last[:, 4 * j : 4 * j + 4] for j in range(3)], axis=0)
    row = lax.broadcasted_iota(jnp.int32, (C, C), 0)
    col = lax.broadcasted_iota(jnp.int32, (C, C), 1)
    for out, j in ((bias1_ref, 0), (bias2_ref, 2)):
        both = four[:, j : j + 1] + four[:, j + 1 : j + 2]
        out[...] = jnp.sum(jnp.where(row == col, both, 0.0), axis=0, keepdims=True)


def out_kernel(count_ref, hid, lo_ref, hi_ref, w2_ref, b2_ref, out_ref, ph, lh, hh, w2s, acc):
    count = count_ref[0, 0]
    masks = lane_masks()
    stack_taps(w2_ref, w2s)
    for i in range(2):
        put_shifts(split(lo_ref[i]), lh, i, masks)
        put_shifts(split(hi_ref[i]), hh, i, masks)
    for p in range(SLOTS):
        put_shifts(split(hid[p]), ph, p, masks)
    conv_local(acc, w2s, ph)
    conv_halo(acc, w2s[0:C, :], lh, 0)
    conv_halo(acc, w2s[2 * C : 3 * C, :], hh, count - 2)
    for p in range(SLOTS):
        keep = jnp.where(p < count, 1.0, 0.0).astype(F32)
        z = ((acc[p] + b2_ref[...]) * keep).astype(BF16)
        for g, part in enumerate(from_halves(split(z), masks)):
            out_ref[0, p, :, 128 * g : 128 * g + 128] = part


TILES = 64
VM = pl.BlockSpec(memory_space=pltpu.VMEM)
SM = pl.BlockSpec(memory_space=pltpu.SMEM)
PAIR_BF16 = jax.ShapeDtypeStruct((2, C, CELLS), BF16)
SHIFTED = jax.ShapeDtypeStruct((SLOTS, ROWS, WIDE), BF16)
SUMS = jax.ShapeDtypeStruct((SLOTS, C, CELLS), F32)
WEIGHT = (ROWS, TAPS9)
MIB = 1024 * 1024


def call(kernel, name, args, outs, scratch, limit, flops, interpret):
    return pl.pallas_call(
        kernel,
        out_shape=outs,
        in_specs=[SM if a.dtype == jnp.int32 else VM for a in args],
        out_specs=[VM] * len(outs),
        scratch_shapes=[pltpu.VMEM(shape, kind) for shape, kind in scratch],
        compiler_params=pltpu.CompilerParams(vmem_limit_bytes=limit * MIB),
        cost_estimate=pl.CostEstimate(flops=flops, bytes_accessed=2_000_000, transcendentals=0),
        interpret=interpret,
        name=name,
    )(*args)


def gradient_sum(tiles, interpret):
    axes = ("box", "snap")
    parts = lax.axis_size(axes)
    rows = TILES * 16 // parts
    shape = (-1, max(rows, 16), 128)
    mine = lax.all_to_all(tiles.reshape(parts, rows, 128), axes, 0, 0, tiled=True).reshape(shape)
    (spread,) = call(
        functools.partial(total_kernel, rows), "total", (mine,),
        (jax.ShapeDtypeStruct(mine.shape, BF16),), [], 4, 1_000_000, interpret,
    )
    spread = spread.reshape(parts, rows, 128)
    return lax.all_to_all(spread, axes, 0, 0, tiled=True).reshape(TILES, 16, 128)


def local(interpret, fields, cotangent, plane_counts, w_first, b_first, w_second, b_second):
    count = plane_counts[0, 0]
    x = fields[0]
    u = cotangent[0]
    size = lax.axis_size("box")
    forward = [(i, i + 1) for i in range(size - 1)]
    backward = [(i + 1, i) for i in range(size - 1)]
    zero = jnp.zeros((), jnp.int32)
    last = lambda v: lax.dynamic_slice(v, (count - 2, zero, zero), (2, C, CELLS))
    lo = lax.ppermute(jnp.concatenate([last(x), last(u)], axis=0), "box", forward)
    hi = lax.ppermute(jnp.concatenate([x[0:2], u[0:2]], axis=0), "box", backward)
    stacked = jax.ShapeDtypeStruct(WEIGHT, BF16)
    px, pu, w1s, w2s, acc1, acc2 = call(
        front_kernel, "front", (plane_counts, x, u, w_first, w_second),
        (SHIFTED, SHIFTED, stacked, stacked, SUMS, SUMS), [], 16, 1_200_000_000, interpret,
    )
    halo = ((2, ROWS, WIDE), BF16)
    low_shape = jax.ShapeDtypeStruct((2, ROWS, WIDE), BF16)
    two = jax.ShapeDtypeStruct((2, C, CELLS), F32)
    lx, lu, two1, two2 = call(
        low_kernel, "low", (w1s, w2s, acc1, acc2, lo),
        (low_shape, low_shape, two, two), [], 16, 300_000_000, interpret,
    )
    hid, head, tail, tiles = call(
        main_kernel, "grads",
        (plane_counts, px, pu, w1s, w2s, acc1, acc2, two1, two2, lx, lu, hi, b_first[:, None]),
        (jax.ShapeDtypeStruct((SLOTS, C, CELLS), BF16), PAIR_BF16, PAIR_BF16, jax.ShapeDtypeStruct((TILES, 16, 128), BF16)),
        [
            ((SLOTS, C, CELLS), F32), ((SLOTS, C, CELLS), F32), ((SLOTS, ROWS, WIDE), BF16),
            halo, halo, ((SLOTS + 4, C, WIDE), BF16), ((SLOTS, C, WIDE), BF16),
            ((TAPS9, ROWS), F32), ((TAPS9, ROWS), F32),
        ],
        32, 2_000_000_000, interpret,
    )
    hid_lo = lax.ppermute(tail, "box", forward)
    hid_hi = lax.ppermute(head, "box", backward)
    tiles = gradient_sum(tiles, interpret)
    (decoded,) = call(
        out_kernel, "decode", (plane_counts, hid, hid_lo, hid_hi, w_second, b_second[:, None]),
        (jax.ShapeDtypeStruct((1, SLOTS, C, CELLS), BF16),),
        [((SLOTS, ROWS, WIDE), BF16), halo, halo, (WEIGHT, BF16), ((SLOTS, C, CELLS), F32)], 24, 1_000_000_000, interpret,
    )
    grad = jax.ShapeDtypeStruct((C, 27 * C), F32)
    line = jax.ShapeDtypeStruct((1, C), F32)
    grad_first, grad_second, bias_first, bias_second = call(
        spread_kernel, "spread", (tiles,), (grad, grad, line, line), [], 8, 100_000_000, interpret,
    )
    return decoded, grad_first, grad_second, bias_first[0], bias_second[0]


def solution(mesh, interpret=False):
    return jax.shard_map(
        functools.partial(local, interpret),
        mesh=mesh,
        in_specs=(
            P("snap", "box", None, None),
            P("snap", "box", None, None),
            P("snap", "box"),
            P(),
            P(),
            P(),
            P(),
        ),
        out_specs=(P("snap", "box", None, None), P(), P(), P(), P()),
        check_vma=False,
    )
```

```python
import functools

import jax
import jax.numpy as jnp
from jax import lax
from jax.experimental import pallas as pl
from jax.experimental.pallas import tpu as pltpu
from jax.sharding import PartitionSpec as P

C = 48
SLOTS = 5
CELLS = 1024
ROWS = 3 * C
TAPS9 = 9 * C
WIDE = CELLS + 256
CHUNK = 256
F32 = jnp.float32
BF16 = jnp.bfloat16


def lane_masks():
    lane = lax.broadcasted_iota(jnp.int32, (C, 128), 1)
    col = lane % 32

    def pick(cond):
        return jnp.where(cond, 1.0, 0.0).astype(BF16)

    return pick(lane < 64), pick(lane >= 64), pick(col >= 2), pick(col < 30)


def roll(v, shift):
    return pltpu.roll(v, shift, 1)


def to_halves(v, masks):
    low, high = masks[:2]
    orig = [v[:, 128 * h : 128 * h + 128] for h in range(8)]
    turned = [roll(o, 64) for o in orig]
    out = []
    for g in range(8):
        m = g // 2
        if g % 2 == 0:
            out.append(orig[m] * low + turned[4 + m] * high)
        else:
            out.append(turned[m] * low + orig[4 + m] * high)
    return out


def from_halves(parts, masks):
    low, high = masks[:2]
    turned = [roll(p, 64) for p in parts]
    first = [parts[2 * m] * low + turned[2 * m + 1] * high for m in range(4)]
    second = [turned[2 * m] * low + parts[2 * m + 1] * high for m in range(4)]
    return first + second


def put_shifts(parts, dst, at, masks):
    low, high, ge2, lt30 = masks
    before = roll(parts[7], 64) * high
    after = roll(parts[0], 64) * low
    for g, t in enumerate([before] + parts + [after]):
        cols = slice(128 * g, 128 * g + 128)
        dst[at, 0:C, cols] = roll(t, 2) * ge2
        dst[at, C : 2 * C, cols] = t
        dst[at, 2 * C : ROWS, cols] = roll(t, 126) * lt30


def split(v):
    return [v[:, 128 * g : 128 * g + 128] for g in range(8)]


def put_zeros(dst, at):
    dst[at] = jnp.zeros((ROWS, WIDE), BF16)


def taps(src, at, start, size):
    return jnp.concatenate(
        [src[at, :, 128 * b + start : 128 * b + start + size] for b in range(3)], axis=0
    )


def outputs_of(q):
    return [(q + 2 - 2 * s, s) for s in range(3) if 0 <= q + 2 - 2 * s < SLOTS]


def conv_local(acc, w, src):
    seen = set()
    for q in range(SLOTS):
        pairs = outputs_of(q)
        lo, hi = pairs[0][1], pairs[-1][1] + 1
        lhs = w[lo * C : hi * C, :]
        for start in range(0, CELLS, CHUNK):
            y = jnp.dot(lhs, taps(src, q, start, CHUNK), preferred_element_type=F32)
            cols = slice(start, start + CHUNK)
            for p, s in pairs:
                piece = y[(s - lo) * C : (s - lo + 1) * C]
                if (p, start) in seen:
                    acc[p, :, cols] += piece
                else:
                    acc[p, :, cols] = piece
                    seen.add((p, start))


def conv_halo(acc, w, src, first):
    for i in range(2):
        for start in range(0, CELLS, CHUNK):
            cols = slice(start, start + CHUNK)
            y = jnp.dot(w, taps(src, i, start, CHUNK), preferred_element_type=F32)
            acc[first + i, :, cols] += y


def lane_dot(a, b):
    return lax.dot_general(a, b, (((1,), (1,)), ((), ())), preferred_element_type=F32)


def padded(parts, masks):
    low, high = masks[:2]
    return [roll(parts[7], 64) * high] + parts + [roll(parts[0], 64) * low]


def rows_of(src, planes):
    pieces = [
        src[p, :, 128 * (2 - b) : 128 * (2 - b) + CELLS] for p in planes for b in range(3)
    ]
    return jnp.concatenate(pieces, axis=0)


def center(src, at):
    return src[at, :, 128 : 128 + CELLS]


def middle(ref, at):
    return ref[at, C : 2 * C, 128 : 128 + CELLS]


def stack_taps(w_ref, dst):
    for s in range(3):
        dst[s * C : (s + 1) * C, :] = w_ref[:, s * TAPS9 : (s + 1) * TAPS9]


def front_kernel(count_ref, x_ref, u_ref, w1_ref, w2_ref, px, pu, w1s, w2s, acc1, acc2):
    count = count_ref[0, 0]
    masks = lane_masks()
    stack_taps(w1_ref, w1s)
    turned = w2_ref[...].astype(F32).T
    for s in range(3):
        rows = [26 - 9 * s - r for r in range(9)]
        w2s[s * C : (s + 1) * C, :] = jnp.concatenate(
            [turned[t * C : (t + 1) * C] for t in rows], axis=1
        ).astype(BF16)
    for p in range(SLOTS):
        keep = jnp.where(p < count, 1.0, 0.0).astype(BF16)
        put_shifts(to_halves(x_ref[p] * keep, masks), px, p, masks)
        put_shifts(to_halves(u_ref[p] * keep, masks), pu, p, masks)
    conv_local(acc1, w1s, px)
    conv_local(acc2, w2s, pu)


def low_kernel(w1s, w2s, acc1, acc2, lo_ref, lx, lu, sum1, sum2):
    masks = lane_masks()
    for i in range(2):
        put_shifts(to_halves(lo_ref[i], masks), lx, i, masks)
        put_shifts(to_halves(lo_ref[2 + i], masks), lu, i, masks)
    for i in range(2):
        sum1[i] = acc1[i]
        sum2[i] = acc2[i]
    conv_halo(sum1, w1s[0:C, :], lx, 0)
    conv_halo(sum2, w2s[0:C, :], lu, 0)


def main_kernel(
    count_ref, px, pu, w1s, w2s, acc1, acc2, two1, two2, lx, lu, hi_ref, b1_ref,
    hid, head_ref, tail_ref, tiles,
    more1, more2, ph, hx, hu, ue, pre, g1, g2,
):
    count = count_ref[0, 0]
    masks = lane_masks()
    for i in range(2):
        put_shifts(to_halves(hi_ref[i], masks), hx, i, masks)
        put_shifts(to_halves(hi_ref[2 + i], masks), hu, i, masks)
    for p in range(SLOTS):
        ue[p + 2] = pu[p, C : 2 * C, :]
    ue[SLOTS + 2] = jnp.zeros((C, WIDE), BF16)
    ue[SLOTS + 3] = jnp.zeros((C, WIDE), BF16)
    for i in range(2):
        ue[i] = lu[i, C : 2 * C, :]
        ue[count + 2 + i] = hu[i, C : 2 * C, :]
    for p in range(SLOTS):
        more1[p] = two1[p] if p < 2 else acc1[p]
        more2[p] = two2[p] if p < 2 else acc2[p]
    conv_halo(more1, w1s[2 * C : 3 * C, :], hx, count - 2)
    conv_halo(more2, w2s[2 * C : 3 * C, :], hu, count - 2)
    bias1 = jnp.zeros((C, 128), F32)
    bias2 = jnp.zeros((C, 128), F32)
    for p in range(SLOTS):
        keep = jnp.where(p < count, 1.0, 0.0).astype(F32)
        parts = []
        grads = []
        for g in range(8):
            cols = slice(128 * g, 128 * g + 128)
            z = more1[p, :, cols] + b1_ref[...]
            sig = 1.0 / (1.0 + jnp.exp(-z))
            parts.append((z * sig * keep).astype(BF16))
            slope = sig * (1.0 + z * (1.0 - sig))
            grad = (more2[p, :, cols] * slope * keep).astype(BF16)
            grads.append(grad)
            bias1 += grad.astype(F32)
            bias2 += pu[p, C : 2 * C, 128 * g + 128 : 128 * g + 256].astype(F32)
        put_shifts(parts, ph, p, masks)
        for g, t in enumerate(padded(grads, masks)):
            pre[p, :, 128 * g : 128 * g + 128] = t
    for p in range(SLOTS):
        hid[p] = middle(ph, p)
    for i in range(2):
        head_ref[i] = middle(ph, i)
        tail_ref[i] = middle(ph, count - 2 + i)
    for q in range(SLOTS):
        y = lane_dot(rows_of(ue, [q + 4, q + 2, q]), center(ph, q))
        if q == 0:
            g2[...] = y
        else:
            g2[...] += y
    g1[...] = jnp.zeros((TAPS9, ROWS), F32)
    for q in range(SLOTS):
        pairs = outputs_of(q)
        lo, hi = pairs[0][1], pairs[-1][1] + 1
        y = lane_dot(rows_of(pre, [p for p, _ in pairs]), center(px, q))
        g1[lo * ROWS : hi * ROWS, :] += y
    for i in range(2):
        g1[0:ROWS, :] += lane_dot(rows_of(pre, [i]), center(lx, i))
        y = lane_dot(rows_of(pre, [count - 2 + i]), center(hx, i))
        g1[2 * ROWS : TAPS9, :] += y
    columns = []
    for bias in (bias1, bias2):
        total = jnp.sum(bias, axis=1, keepdims=True)
        high = total.astype(BF16).astype(F32)
        columns += [high, total - high]
    ends = []
    for r in range(54):
        src, row = (g1, r * 16) if r < 27 else (g2, r * 16 - TAPS9)
        tiles[r] = src[row : row + 16, 0:128].astype(BF16)
        ends.append(src[row : row + 16, 128:ROWS].astype(BF16))
    ends += [jnp.zeros((16, 16), BF16)] * 2
    for j in range(7):
        tiles[54 + j] = jnp.concatenate(ends[8 * j : 8 * j + 8], axis=1)
    four = jnp.concatenate(columns, axis=1)
    row = [four[16 * j : 16 * j + 16] for j in range(3)] + [jnp.zeros((16, 116), F32)]
    tiles[61] = jnp.concatenate(row, axis=1).astype(BF16)
    tiles[62] = jnp.zeros((16, 128), BF16)
    tiles[63] = jnp.zeros((16, 128), BF16)


def total_kernel(rows, src, out):
    total = src[0].astype(F32)
    for i in range(1, src.shape[0]):
        total += src[i].astype(F32)
    copies = total.shape[0] // rows
    part = total[0:rows]
    for i in range(1, copies):
        part += total[i * rows : (i + 1) * rows]
    block = jnp.concatenate([part] * copies, axis=0).astype(BF16)
    for i in range(out.shape[0]):
        out[i] = block


def spread_kernel(tiles, g1_ref, g2_ref, bias1_ref, bias2_ref):
    for r in range(6):
        pieces = []
        for n in range(9):
            t = (r // 3) * 27 + n * 3 + r % 3
            pieces += [tiles[t], tiles[54 + t // 8, :, 16 * (t % 8) : 16 * (t % 8) + 16]]
        out = g1_ref if r < 3 else g2_ref
        row = (r % 3) * 16
        out[row : row + 16, :] = jnp.concatenate(pieces, axis=1).astype(F32)
    last = tiles[61].astype(F32)
    four = jnp.concatenate([last[:, 4 * j : 4 * j + 4] for j in range(3)], axis=0)
    row = lax.broadcasted_iota(jnp.int32, (C, C), 0)
    col = lax.broadcasted_iota(jnp.int32, (C, C), 1)
    for out, j in ((bias1_ref, 0), (bias2_ref, 2)):
        both = four[:, j : j + 1] + four[:, j + 1 : j + 2]
        out[...] = jnp.sum(jnp.where(row == col, both, 0.0), axis=0, keepdims=True)


def inner_kernel(hid, w2_ref, w2s, acc, ph):
    masks = lane_masks()
    stack_taps(w2_ref, w2s)
    for p in range(SLOTS):
        put_shifts(split(hid[p]), ph, p, masks)
    conv_local(acc, w2s, ph)


def out_kernel(count_ref, w2s, inner, lo_ref, hi_ref, b2_ref, out_ref, lh, hh, acc):
    count = count_ref[0, 0]
    masks = lane_masks()
    for p in range(SLOTS):
        acc[p] = inner[p]
    for i in range(2):
        put_shifts(split(lo_ref[i]), lh, i, masks)
        put_shifts(split(hi_ref[i]), hh, i, masks)
    conv_halo(acc, w2s[0:C, :], lh, 0)
    conv_halo(acc, w2s[2 * C : 3 * C, :], hh, count - 2)
    for p in range(SLOTS):
        keep = jnp.where(p < count, 1.0, 0.0).astype(F32)
        z = ((acc[p] + b2_ref[...]) * keep).astype(BF16)
        for g, part in enumerate(from_halves(split(z), masks)):
            out_ref[0, p, :, 128 * g : 128 * g + 128] = part


TILES = 64
VM = pl.BlockSpec(memory_space=pltpu.VMEM)
SM = pl.BlockSpec(memory_space=pltpu.SMEM)
PAIR_BF16 = jax.ShapeDtypeStruct((2, C, CELLS), BF16)
SHIFTED = jax.ShapeDtypeStruct((SLOTS, ROWS, WIDE), BF16)
SUMS = jax.ShapeDtypeStruct((SLOTS, C, CELLS), F32)
WEIGHT = (ROWS, TAPS9)
MIB = 1024 * 1024


def call(kernel, name, args, outs, scratch, limit, flops, interpret):
    return pl.pallas_call(
        kernel,
        out_shape=outs,
        in_specs=[SM if a.dtype == jnp.int32 else VM for a in args],
        out_specs=[VM] * len(outs),
        scratch_shapes=[pltpu.VMEM(shape, kind) for shape, kind in scratch],
        compiler_params=pltpu.CompilerParams(vmem_limit_bytes=limit * MIB),
        cost_estimate=pl.CostEstimate(flops=flops, bytes_accessed=2_000_000, transcendentals=0),
        interpret=interpret,
        name=name,
    )(*args)


def gradient_sum(tiles, interpret):
    axes = ("box", "snap")
    parts = lax.axis_size(axes)
    rows = TILES * 16 // parts
    shape = (-1, max(rows, 16), 128)
    mine = lax.all_to_all(tiles.reshape(parts, rows, 128), axes, 0, 0, tiled=True).reshape(shape)
    (spread,) = call(
        functools.partial(total_kernel, rows), "total", (mine,),
        (jax.ShapeDtypeStruct(mine.shape, BF16),), [], 4, 1_000_000, interpret,
    )
    spread = spread.reshape(parts, rows, 128)
    return lax.all_to_all(spread, axes, 0, 0, tiled=True).reshape(TILES, 16, 128)


def local(interpret, fields, cotangent, plane_counts, w_first, b_first, w_second, b_second):
    count = plane_counts[0, 0]
    x = fields[0]
    u = cotangent[0]
    size = lax.axis_size("box")
    forward = [(i, i + 1) for i in range(size - 1)]
    backward = [(i + 1, i) for i in range(size - 1)]
    zero = jnp.zeros((), jnp.int32)
    last = lambda v: lax.dynamic_slice(v, (count - 2, zero, zero), (2, C, CELLS))
    lo = lax.ppermute(jnp.concatenate([last(x), last(u)], axis=0), "box", forward)
    hi = lax.ppermute(jnp.concatenate([x[0:2], u[0:2]], axis=0), "box", backward)
    stacked = jax.ShapeDtypeStruct(WEIGHT, BF16)
    px, pu, w1s, w2s, acc1, acc2 = call(
        front_kernel, "front", (plane_counts, x, u, w_first, w_second),
        (SHIFTED, SHIFTED, stacked, stacked, SUMS, SUMS), [], 16, 1_200_000_000, interpret,
    )
    halo = ((2, ROWS, WIDE), BF16)
    low_shape = jax.ShapeDtypeStruct((2, ROWS, WIDE), BF16)
    two = jax.ShapeDtypeStruct((2, C, CELLS), F32)
    lx, lu, two1, two2 = call(
        low_kernel, "low", (w1s, w2s, acc1, acc2, lo),
        (low_shape, low_shape, two, two), [], 16, 300_000_000, interpret,
    )
    hid, head, tail, tiles = call(
        main_kernel, "grads",
        (plane_counts, px, pu, w1s, w2s, acc1, acc2, two1, two2, lx, lu, hi, b_first[:, None]),
        (jax.ShapeDtypeStruct((SLOTS, C, CELLS), BF16), PAIR_BF16, PAIR_BF16, jax.ShapeDtypeStruct((TILES, 16, 128), BF16)),
        [
            ((SLOTS, C, CELLS), F32), ((SLOTS, C, CELLS), F32), ((SLOTS, ROWS, WIDE), BF16),
            halo, halo, ((SLOTS + 4, C, WIDE), BF16), ((SLOTS, C, WIDE), BF16),
            ((TAPS9, ROWS), F32), ((TAPS9, ROWS), F32),
        ],
        32, 2_000_000_000, interpret,
    )
    hid_lo = lax.ppermute(tail, "box", forward)
    hid_hi = lax.ppermute(head, "box", backward)
    tiles = gradient_sum(tiles, interpret)
    second, inner = call(
        inner_kernel, "inner", (hid, w_second), (stacked, SUMS),
        [((SLOTS, ROWS, WIDE), BF16)], 16, 1_000_000_000, interpret,
    )
    (decoded,) = call(
        out_kernel, "decode", (plane_counts, second, inner, hid_lo, hid_hi, b_second[:, None]),
        (jax.ShapeDtypeStruct((1, SLOTS, C, CELLS), BF16),),
        [halo, halo, ((SLOTS, C, CELLS), F32)], 16, 300_000_000, interpret,
    )
    grad = jax.ShapeDtypeStruct((C, 27 * C), F32)
    line = jax.ShapeDtypeStruct((1, C), F32)
    grad_first, grad_second, bias_first, bias_second = call(
        spread_kernel, "spread", (tiles,), (grad, grad, line, line), [], 8, 100_000_000, interpret,
    )
    return decoded, grad_first, grad_second, bias_first[0], bias_second[0]


def solution(mesh, interpret=False):
    return jax.shard_map(
        functools.partial(local, interpret),
        mesh=mesh,
        in_specs=(
            P("snap", "box", None, None),
            P("snap", "box", None, None),
            P("snap", "box"),
            P(),
            P(),
            P(),
            P(),
        ),
        out_specs=(P("snap", "box", None, None), P(), P(), P(), P()),
        check_vma=False,
    )
```

```python
import functools

import jax
import jax.numpy as jnp
from jax import lax
from jax.experimental import pallas as pl
from jax.experimental.pallas import tpu as pltpu
from jax.sharding import PartitionSpec as P

C = 48
SLOTS = 5
CELLS = 1024
ROWS = 3 * C
TAPS9 = 9 * C
WIDE = CELLS + 256
CHUNK = 256
F32 = jnp.float32
BF16 = jnp.bfloat16


def lane_masks():
    lane = lax.broadcasted_iota(jnp.int32, (C, 128), 1)
    col = lane % 32

    def pick(cond):
        return jnp.where(cond, 1.0, 0.0).astype(BF16)

    return pick(lane < 64), pick(lane >= 64), pick(col >= 2), pick(col < 30)


def roll(v, shift):
    return pltpu.roll(v, shift, 1)


def to_halves(v, masks):
    low, high = masks[:2]
    orig = [v[:, 128 * h : 128 * h + 128] for h in range(8)]
    turned = [roll(o, 64) for o in orig]
    out = []
    for g in range(8):
        m = g // 2
        if g % 2 == 0:
            out.append(orig[m] * low + turned[4 + m] * high)
        else:
            out.append(turned[m] * low + orig[4 + m] * high)
    return out


def from_halves(parts, masks):
    low, high = masks[:2]
    turned = [roll(p, 64) for p in parts]
    first = [parts[2 * m] * low + turned[2 * m + 1] * high for m in range(4)]
    second = [turned[2 * m] * low + parts[2 * m + 1] * high for m in range(4)]
    return first + second


def put_shifts(parts, dst, at, masks):
    low, high, ge2, lt30 = masks
    before = roll(parts[7], 64) * high
    after = roll(parts[0], 64) * low
    for g, t in enumerate([before] + parts + [after]):
        cols = slice(128 * g, 128 * g + 128)
        dst[at, 0:C, cols] = roll(t, 2) * ge2
        dst[at, C : 2 * C, cols] = t
        dst[at, 2 * C : ROWS, cols] = roll(t, 126) * lt30


def split(v):
    return [v[:, 128 * g : 128 * g + 128] for g in range(8)]


def put_zeros(dst, at):
    dst[at] = jnp.zeros((ROWS, WIDE), BF16)


def taps(src, at, start, size):
    return jnp.concatenate(
        [src[at, :, 128 * b + start : 128 * b + start + size] for b in range(3)], axis=0
    )


def outputs_of(q):
    return [(q + 2 - 2 * s, s) for s in range(3) if 0 <= q + 2 - 2 * s < SLOTS]


def conv_local(acc, w, src):
    seen = set()
    for q in range(SLOTS):
        pairs = outputs_of(q)
        lo, hi = pairs[0][1], pairs[-1][1] + 1
        lhs = w[lo * C : hi * C, :]
        for start in range(0, CELLS, CHUNK):
            y = jnp.dot(lhs, taps(src, q, start, CHUNK), preferred_element_type=F32)
            cols = slice(start, start + CHUNK)
            for p, s in pairs:
                piece = y[(s - lo) * C : (s - lo + 1) * C]
                if (p, start) in seen:
                    acc[p, :, cols] += piece
                else:
                    acc[p, :, cols] = piece
                    seen.add((p, start))


def conv_halo(acc, w, src, first):
    for i in range(2):
        for start in range(0, CELLS, CHUNK):
            cols = slice(start, start + CHUNK)
            y = jnp.dot(w, taps(src, i, start, CHUNK), preferred_element_type=F32)
            acc[first + i, :, cols] += y


def lane_dot(a, b):
    return lax.dot_general(a, b, (((1,), (1,)), ((), ())), preferred_element_type=F32)


def padded(parts, masks):
    low, high = masks[:2]
    return [roll(parts[7], 64) * high] + parts + [roll(parts[0], 64) * low]


def rows_of(src, planes):
    pieces = [
        src[p, :, 128 * (2 - b) : 128 * (2 - b) + CELLS] for p in planes for b in range(3)
    ]
    return jnp.concatenate(pieces, axis=0)


def center(src, at):
    return src[at, :, 128 : 128 + CELLS]


def middle(ref, at):
    return ref[at, C : 2 * C, 128 : 128 + CELLS]


def stack_taps(w_ref, dst):
    for s in range(3):
        dst[s * C : (s + 1) * C, :] = w_ref[:, s * TAPS9 : (s + 1) * TAPS9]


def front_kernel(count_ref, x_ref, u_ref, w1_ref, w2_ref, px, pu, w1s, w2s, acc1, acc2):
    count = count_ref[0, 0]
    masks = lane_masks()
    stack_taps(w1_ref, w1s)
    turned = w2_ref[...].astype(F32).T
    for s in range(3):
        rows = [26 - 9 * s - r for r in range(9)]
        w2s[s * C : (s + 1) * C, :] = jnp.concatenate(
            [turned[t * C : (t + 1) * C] for t in rows], axis=1
        ).astype(BF16)
    for p in range(SLOTS):
        keep = jnp.where(p < count, 1.0, 0.0).astype(BF16)
        put_shifts(to_halves(x_ref[p] * keep, masks), px, p, masks)
        put_shifts(to_halves(u_ref[p] * keep, masks), pu, p, masks)
    conv_local(acc1, w1s, px)
    conv_local(acc2, w2s, pu)


def low_kernel(w1s, w2s, acc1, acc2, lo_ref, lx, lu, sum1, sum2):
    masks = lane_masks()
    for i in range(2):
        put_shifts(to_halves(lo_ref[i], masks), lx, i, masks)
        put_shifts(to_halves(lo_ref[2 + i], masks), lu, i, masks)
    for i in range(2):
        sum1[i] = acc1[i]
        sum2[i] = acc2[i]
    conv_halo(sum1, w1s[0:C, :], lx, 0)
    conv_halo(sum2, w2s[0:C, :], lu, 0)


def main_kernel(
    count_ref, px, pu, w1s, w2s, acc1, acc2, two1, two2, lx, lu, hi_ref, b1_ref,
    hid, head_ref, tail_ref, tiles,
    more1, more2, ph, hx, hu, ue, pre, g1, g2,
):
    count = count_ref[0, 0]
    masks = lane_masks()
    for i in range(2):
        put_shifts(to_halves(hi_ref[i], masks), hx, i, masks)
        put_shifts(to_halves(hi_ref[2 + i], masks), hu, i, masks)
    for p in range(SLOTS):
        ue[p + 2] = pu[p, C : 2 * C, :]
    ue[SLOTS + 2] = jnp.zeros((C, WIDE), BF16)
    ue[SLOTS + 3] = jnp.zeros((C, WIDE), BF16)
    for i in range(2):
        ue[i] = lu[i, C : 2 * C, :]
        ue[count + 2 + i] = hu[i, C : 2 * C, :]
    for p in range(SLOTS):
        more1[p] = two1[p] if p < 2 else acc1[p]
        more2[p] = two2[p] if p < 2 else acc2[p]
    conv_halo(more1, w1s[2 * C : 3 * C, :], hx, count - 2)
    conv_halo(more2, w2s[2 * C : 3 * C, :], hu, count - 2)
    bias1 = jnp.zeros((C, 128), F32)
    bias2 = jnp.zeros((C, 128), F32)
    for p in range(SLOTS):
        keep = jnp.where(p < count, 1.0, 0.0).astype(F32)
        parts = []
        grads = []
        for g in range(8):
            cols = slice(128 * g, 128 * g + 128)
            z = more1[p, :, cols] + b1_ref[...]
            sig = 1.0 / (1.0 + jnp.exp(-z))
            parts.append((z * sig * keep).astype(BF16))
            slope = sig * (1.0 + z * (1.0 - sig))
            grad = (more2[p, :, cols] * slope * keep).astype(BF16)
            grads.append(grad)
            bias1 += grad.astype(F32)
            bias2 += pu[p, C : 2 * C, 128 * g + 128 : 128 * g + 256].astype(F32)
        put_shifts(parts, ph, p, masks)
        for g, t in enumerate(padded(grads, masks)):
            pre[p, :, 128 * g : 128 * g + 128] = t
    for p in range(SLOTS):
        hid[p] = middle(ph, p)
    for i in range(2):
        head_ref[i] = middle(ph, i)
        tail_ref[i] = middle(ph, count - 2 + i)
    for q in range(SLOTS):
        y = lane_dot(rows_of(ue, [q + 4, q + 2, q]), center(ph, q))
        if q == 0:
            g2[...] = y
        else:
            g2[...] += y
    g1[...] = jnp.zeros((TAPS9, ROWS), F32)
    for q in range(SLOTS):
        pairs = outputs_of(q)
        lo, hi = pairs[0][1], pairs[-1][1] + 1
        y = lane_dot(rows_of(pre, [p for p, _ in pairs]), center(px, q))
        g1[lo * ROWS : hi * ROWS, :] += y
    for i in range(2):
        g1[0:ROWS, :] += lane_dot(rows_of(pre, [i]), center(lx, i))
        y = lane_dot(rows_of(pre, [count - 2 + i]), center(hx, i))
        g1[2 * ROWS : TAPS9, :] += y
    columns = []
    for bias in (bias1, bias2):
        total = jnp.sum(bias, axis=1, keepdims=True)
        high = total.astype(BF16).astype(F32)
        columns += [high, total - high]
    ends = []
    for r in range(54):
        src, row = (g1, r * 16) if r < 27 else (g2, r * 16 - TAPS9)
        tiles[r] = src[row : row + 16, 0:128].astype(BF16)
        ends.append(src[row : row + 16, 128:ROWS].astype(BF16))
    ends += [jnp.zeros((16, 16), BF16)] * 2
    for j in range(7):
        tiles[54 + j] = jnp.concatenate(ends[8 * j : 8 * j + 8], axis=1)
    four = jnp.concatenate(columns, axis=1)
    row = [four[16 * j : 16 * j + 16] for j in range(3)] + [jnp.zeros((16, 116), F32)]
    tiles[61] = jnp.concatenate(row, axis=1).astype(BF16)
    tiles[62] = jnp.zeros((16, 128), BF16)
    tiles[63] = jnp.zeros((16, 128), BF16)


def total_kernel(rows, src, out):
    total = src[0].astype(F32)
    for i in range(1, src.shape[0]):
        total += src[i].astype(F32)
    copies = total.shape[0] // rows
    part = total[0:rows]
    for i in range(1, copies):
        part += total[i * rows : (i + 1) * rows]
    block = jnp.concatenate([part] * copies, axis=0).astype(BF16)
    for i in range(out.shape[0]):
        out[i] = block


def spread_kernel(tiles, g1_ref, g2_ref, bias1_ref, bias2_ref):
    for r in range(6):
        pieces = []
        for n in range(9):
            t = (r // 3) * 27 + n * 3 + r % 3
            pieces += [tiles[t], tiles[54 + t // 8, :, 16 * (t % 8) : 16 * (t % 8) + 16]]
        out = g1_ref if r < 3 else g2_ref
        row = (r % 3) * 16
        out[row : row + 16, :] = jnp.concatenate(pieces, axis=1).astype(F32)
    last = tiles[61].astype(F32)
    four = jnp.concatenate([last[:, 4 * j : 4 * j + 4] for j in range(3)], axis=0)
    row = lax.broadcasted_iota(jnp.int32, (C, C), 0)
    col = lax.broadcasted_iota(jnp.int32, (C, C), 1)
    for out, j in ((bias1_ref, 0), (bias2_ref, 2)):
        both = four[:, j : j + 1] + four[:, j + 1 : j + 2]
        out[...] = jnp.sum(jnp.where(row == col, both, 0.0), axis=0, keepdims=True)


def inner_kernel(hid, w2_ref, w2s, acc, ph):
    masks = lane_masks()
    stack_taps(w2_ref, w2s)
    for p in range(SLOTS):
        put_shifts(split(hid[p]), ph, p, masks)
    conv_local(acc, w2s, ph)


def edge_kernel(w2s, inner, lo_ref, two, lh):
    masks = lane_masks()
    for i in range(2):
        put_shifts(split(lo_ref[i]), lh, i, masks)
        two[i] = inner[i]
    conv_halo(two, w2s[0:C, :], lh, 0)


def out_kernel(count_ref, w2s, inner, two, hi_ref, b2_ref, out_ref, hh, acc):
    count = count_ref[0, 0]
    masks = lane_masks()
    for p in range(SLOTS):
        acc[p] = two[p] if p < 2 else inner[p]
    for i in range(2):
        put_shifts(split(hi_ref[i]), hh, i, masks)
    conv_halo(acc, w2s[2 * C : 3 * C, :], hh, count - 2)
    for p in range(SLOTS):
        keep = jnp.where(p < count, 1.0, 0.0).astype(F32)
        z = ((acc[p] + b2_ref[...]) * keep).astype(BF16)
        for g, part in enumerate(from_halves(split(z), masks)):
            out_ref[0, p, :, 128 * g : 128 * g + 128] = part


TILES = 64
VM = pl.BlockSpec(memory_space=pltpu.VMEM)
SM = pl.BlockSpec(memory_space=pltpu.SMEM)
PAIR_BF16 = jax.ShapeDtypeStruct((2, C, CELLS), BF16)
SHIFTED = jax.ShapeDtypeStruct((SLOTS, ROWS, WIDE), BF16)
SUMS = jax.ShapeDtypeStruct((SLOTS, C, CELLS), F32)
WEIGHT = (ROWS, TAPS9)
MIB = 1024 * 1024


def call(kernel, name, args, outs, scratch, limit, flops, interpret):
    return pl.pallas_call(
        kernel,
        out_shape=outs,
        in_specs=[SM if a.dtype == jnp.int32 else VM for a in args],
        out_specs=[VM] * len(outs),
        scratch_shapes=[pltpu.VMEM(shape, kind) for shape, kind in scratch],
        compiler_params=pltpu.CompilerParams(vmem_limit_bytes=limit * MIB),
        cost_estimate=pl.CostEstimate(flops=flops, bytes_accessed=2_000_000, transcendentals=0),
        interpret=interpret,
        name=name,
    )(*args)


def gradient_sum(tiles, interpret):
    axes = ("box", "snap")
    parts = lax.axis_size(axes)
    rows = TILES * 16 // parts
    shape = (-1, max(rows, 16), 128)
    mine = lax.all_to_all(tiles.reshape(parts, rows, 128), axes, 0, 0, tiled=True).reshape(shape)
    (spread,) = call(
        functools.partial(total_kernel, rows), "total", (mine,),
        (jax.ShapeDtypeStruct(mine.shape, BF16),), [], 4, 1_000_000, interpret,
    )
    spread = spread.reshape(parts, rows, 128)
    return lax.all_to_all(spread, axes, 0, 0, tiled=True).reshape(TILES, 16, 128)


def local(interpret, fields, cotangent, plane_counts, w_first, b_first, w_second, b_second):
    count = plane_counts[0, 0]
    x = fields[0]
    u = cotangent[0]
    size = lax.axis_size("box")
    forward = [(i, i + 1) for i in range(size - 1)]
    backward = [(i + 1, i) for i in range(size - 1)]
    zero = jnp.zeros((), jnp.int32)
    last = lambda v: lax.dynamic_slice(v, (count - 2, zero, zero), (2, C, CELLS))
    lo = lax.ppermute(jnp.concatenate([last(x), last(u)], axis=0), "box", forward)
    hi = lax.ppermute(jnp.concatenate([x[0:2], u[0:2]], axis=0), "box", backward)
    stacked = jax.ShapeDtypeStruct(WEIGHT, BF16)
    px, pu, w1s, w2s, acc1, acc2 = call(
        front_kernel, "front", (plane_counts, x, u, w_first, w_second),
        (SHIFTED, SHIFTED, stacked, stacked, SUMS, SUMS), [], 16, 1_200_000_000, interpret,
    )
    halo = ((2, ROWS, WIDE), BF16)
    low_shape = jax.ShapeDtypeStruct((2, ROWS, WIDE), BF16)
    two = jax.ShapeDtypeStruct((2, C, CELLS), F32)
    lx, lu, two1, two2 = call(
        low_kernel, "low", (w1s, w2s, acc1, acc2, lo),
        (low_shape, low_shape, two, two), [], 16, 300_000_000, interpret,
    )
    hid, head, tail, tiles = call(
        main_kernel, "grads",
        (plane_counts, px, pu, w1s, w2s, acc1, acc2, two1, two2, lx, lu, hi, b_first[:, None]),
        (jax.ShapeDtypeStruct((SLOTS, C, CELLS), BF16), PAIR_BF16, PAIR_BF16, jax.ShapeDtypeStruct((TILES, 16, 128), BF16)),
        [
            ((SLOTS, C, CELLS), F32), ((SLOTS, C, CELLS), F32), ((SLOTS, ROWS, WIDE), BF16),
            halo, halo, ((SLOTS + 4, C, WIDE), BF16), ((SLOTS, C, WIDE), BF16),
            ((TAPS9, ROWS), F32), ((TAPS9, ROWS), F32),
        ],
        32, 2_000_000_000, interpret,
    )
    hid_lo = lax.ppermute(tail, "box", forward)
    hid_hi = lax.ppermute(head, "box", backward)
    tiles = gradient_sum(tiles, interpret)
    second, inner = call(
        inner_kernel, "inner", (hid, w_second), (stacked, SUMS),
        [((SLOTS, ROWS, WIDE), BF16)], 16, 1_000_000_000, interpret,
    )
    (edge,) = call(
        edge_kernel, "edge", (second, inner, hid_lo), (two,), [halo], 8, 200_000_000, interpret
    )
    (decoded,) = call(
        out_kernel, "decode", (plane_counts, second, inner, edge, hid_hi, b_second[:, None]),
        (jax.ShapeDtypeStruct((1, SLOTS, C, CELLS), BF16),),
        [halo, ((SLOTS, C, CELLS), F32)], 16, 300_000_000, interpret,
    )
    grad = jax.ShapeDtypeStruct((C, 27 * C), F32)
    line = jax.ShapeDtypeStruct((1, C), F32)
    grad_first, grad_second, bias_first, bias_second = call(
        spread_kernel, "spread", (tiles,), (grad, grad, line, line), [], 8, 100_000_000, interpret,
    )
    return decoded, grad_first, grad_second, bias_first[0], bias_second[0]


def solution(mesh, interpret=False):
    return jax.shard_map(
        functools.partial(local, interpret),
        mesh=mesh,
        in_specs=(
            P("snap", "box", None, None),
            P("snap", "box", None, None),
            P("snap", "box"),
            P(),
            P(),
            P(),
            P(),
        ),
        out_specs=(P("snap", "box", None, None), P(), P(), P(), P()),
        check_vma=False,
    )
```
